32 devices in a mesh: seq: 8 (over z, y), head: 4 (over x, core).
Axes of the slice: x: 2, y: 2, z: 4, core: 2. Of those that a mesh axis runs over, the one named last changes fastest.
Arguments:
- tokens: bfloat16 [8192, 2048], P('seq'), may hold values from -6 to 6
- w_query: bfloat16 [2048, 2048], P(None, 'head'), may hold values from -0.125 to 0.125
- w_key: bfloat16 [2048, 2048], P(None, 'head'), may hold values from -0.125 to 0.125
- w_value: bfloat16 [2048, 2048], P(None, 'head'), may hold values from -0.125 to 0.125
- omega: float32 [128, 256], replicated, may hold values from -5 to 5
- w_out: bfloat16 [2048, 2048], P('head'), may hold values from -0.125 to 0.125
Outputs:
- mixed: bfloat16 [8192, 2048], P(('seq', 'head'))
The draws below stay inside these ranges and needn't reach their ends.
All inputs are finite; a program needn't handle non-finite values.
Results may differ from the reference program's by a relative error of at most 0.0063.
Values may be sent and summed in bfloat16 or wider, within the bound.
No kernel may reach another device: no remote copies, remote signals or barrier semaphores. Data moves between devices by JAX's collectives and lax.ppermute only.
A program may use at most 128 MiB of HBM per device.

```python
import math
import jax
import jax.numpy as jnp
from jax import lax

D = 2048
HEADS = 16
DH = 128
M = 256
BLOCK = 512
TOKENS = 8192


def block_levels(stream_key, dims, cuts, least, top_value):
    gain = 1.0
    for axis_at, blocks in cuts:
        heights = jax.random.uniform(jax.random.fold_in(jax.random.fold_in(stream_key, 6), axis_at), (blocks,), jnp.float32, least / len(cuts), top_value / len(cuts))
        gain = gain * jnp.repeat(jnp.exp(heights), dims[axis_at] // blocks).reshape((-1,) + (1,) * (len(dims) - 1 - axis_at))
    return gain


def gaussian(rng, extent, deviation, bound, cuts=(), kind=jnp.bfloat16):
    level = block_levels(rng, extent, cuts, -0.22, 0.18) if cuts else 1.0
    entries = jax.random.normal(rng, extent, jnp.float32) * deviation * level
    return jnp.minimum(jnp.maximum(entries, -bound), bound).astype(kind)


def setup_inputs(seed: int = 0) -> dict:
    splits = jax.random.split(jax.random.key(seed), 7)
    return {
        "tokens": gaussian(splits[0], (TOKENS, D), 1.0, 6.0, ((0, 8),)),
        "w_query": gaussian(splits[1], (D, HEADS * DH), D ** -0.5, 0.125, ((1, 4),)),
        "w_key": gaussian(splits[2], (D, HEADS * DH), D ** -0.5, 0.125, ((1, 4),)),
        "w_value": gaussian(splits[3], (D, HEADS * DH), D ** -0.5, 0.125, ((1, 4),)),
        "omega": gaussian(splits[4], (DH, M), 1.0, 5.0, (), jnp.float32),
        "w_out": gaussian(splits[5], (HEADS * DH, D), (HEADS * DH) ** -0.5, 0.125, ((0, 4),)),
    }


highest_precision = lax.Precision.HIGHEST
stabilizer = 0.001

def feature_map(values, omega):
    scaled = values * DH ** (-0.25)
    projected = jnp.einsum('thd,dm->thm', scaled, omega, precision=highest_precision)
    half_square = 0.5 * lax.optimization_barrier(jnp.sum(scaled * scaled, axis=-1, keepdims=True))
    return ((jnp.exp(projected - half_square) + stabilizer) / math.sqrt(M)).astype(jnp.bfloat16)

def reference(tokens, w_query, w_key, w_value, omega, w_out):
    length = tokens.shape[0]
    query = jnp.dot(tokens, w_query, preferred_element_type=jnp.float32).reshape(length, HEADS, DH)
    key = jnp.dot(tokens, w_key, preferred_element_type=jnp.float32).reshape(length, HEADS, DH)
    value = jnp.dot(tokens, w_value, preferred_element_type=jnp.float32).astype(jnp.bfloat16).reshape(length, HEADS, DH)
    query_feat = feature_map(query, omega)
    key_feat = feature_map(key, omega)
    block_count = length // BLOCK
    query_blocks = query_feat.reshape(block_count, BLOCK, HEADS, M)
    key_blocks = key_feat.reshape(block_count, BLOCK, HEADS, M)
    value_blocks = value.reshape(block_count, BLOCK, HEADS, DH)
    causal = jnp.arange(BLOCK)[:, None] >= jnp.arange(BLOCK)[None, :]

    def advance(carry, blocks):
        state_matrix, norm = carry
        query_features = blocks[0].astype(jnp.float32)
        key_features = blocks[1].astype(jnp.float32)
        value_features = blocks[2].astype(jnp.float32)
        scores = jnp.einsum('thm,shm->hts', query_features, key_features, precision=highest_precision)
        scores = jnp.where(causal[None], scores, jnp.float32(0.0))
        denom = lax.optimization_barrier(jnp.sum(scores, axis=-1)).T + jnp.einsum('thm,hm->th', query_features, norm, precision=highest_precision)
        weights = lax.optimization_barrier(scores.astype(jnp.bfloat16)).astype(jnp.float32)
        numerator = jnp.einsum('hts,shd->thd', weights, value_features, precision=highest_precision)
        numerator = numerator + jnp.einsum('crx,rxs->crs', query_features, state_matrix, precision=highest_precision)
        attended = (numerator / denom[..., None]).astype(jnp.bfloat16)
        state_matrix = state_matrix + jnp.einsum('xtv,xte->tve', key_features, value_features, precision=highest_precision)
        norm = norm + lax.optimization_barrier(jnp.sum(key_features, axis=0))
        return ((state_matrix, norm), attended)
    start_state = (jnp.zeros((HEADS, M, DH), jnp.float32), jnp.zeros((HEADS, M), jnp.float32))
    ignored, attended = lax.scan(advance, start_state, (query_blocks, key_blocks, value_blocks))
    attention = attended.reshape(length, HEADS * DH)
    return jnp.dot(attention, w_out, preferred_element_type=jnp.float32).astype(jnp.bfloat16)
```

```python
import functools
import math

import jax
import jax.numpy as jnp
from jax import lax
from jax.experimental import pallas as pl
from jax.experimental.pallas import tpu as pltpu
from jax.sharding import PartitionSpec as P

BLOCK = 512
TAIL = 16
STABILIZER = 0.001
BF16 = jnp.bfloat16
F32 = jnp.float32


def params(mib):
    return pltpu.CompilerParams(vmem_limit_bytes=mib * 2**20)


def dot(a, b):
    return lax.dot_general(a, b, (((1,), (0,)), ((), ())), preferred_element_type=F32)


def dot_nt(a, b):
    return lax.dot_general(a, b, (((1,), (1,)), ((), ())), preferred_element_type=F32)


def dot_tn(a, b):
    return lax.dot_general(a, b, (((0,), (0,)), ((), ())), preferred_element_type=F32)


def halves(value):
    high = value.astype(BF16)
    return high, (value - high.astype(F32)).astype(BF16)


def feature_weights(omega):
    size, features = omega.shape
    high, low = halves(omega * size ** (-0.25))
    minus = jnp.full((2 * size, features), -1.0, BF16)
    return jnp.concatenate([high, high, low, low, minus], axis=0)


def features(rows, weights):
    size = rows.shape[1]
    high, low = halves(rows)
    square_high, square_low = halves(rows * rows * (0.5 * size ** (-0.5)))
    left = jnp.concatenate([high, low, high, low, square_high, square_low], axis=1)
    exponent = dot(left, weights)
    return ((jnp.exp(exponent) + STABILIZER) * (1.0 / math.sqrt(weights.shape[1]))).astype(BF16)


def key_kernel(tok, wk, wv, omega, feat, value, state, message, local):
    block = pl.program_id(1)
    size = omega.shape[0]
    weights = feature_weights(omega[...])
    keys = dot(tok[...], wk[...])
    values = dot(tok[...], wv[...]).astype(BF16)
    value[...] = values
    for j in range(feat.shape[0]):
        f = features(keys[:, j * size : (j + 1) * size], weights)
        feat[j] = f
        outer = dot_tn(values[:, j * size : (j + 1) * size], f)
        norm = jnp.sum(f.astype(F32), axis=0, keepdims=True)
        added = jnp.concatenate([outer, norm, jnp.zeros((TAIL - 1, f.shape[1]), F32)], axis=0)

        @pl.when(block == 0)
        def _():
            state[j] = added

        @pl.when(block > 0)
        def _():
            state[j] += added

        total = state[j]
        norm = total[size : size + 1]
        high, low = halves(norm)
        message[j] = jnp.concatenate(
            [total[:size].astype(BF16), high, low, jnp.zeros((TAIL - 2, f.shape[1]), BF16)], axis=0
        )
        local[0, j] = jnp.concatenate(
            [total[:size].astype(BF16), jnp.broadcast_to(high, (size, f.shape[1]))], axis=0
        )


def query_kernel(tok, wq, omega, feat, value, local, qfeat, result):
    block = pl.program_id(1)
    size = omega.shape[0]
    rows = tok.shape[0]
    half = rows // 2
    weights = feature_weights(omega[...])
    query = dot(tok[...], wq[...])
    causal = lax.broadcasted_iota(jnp.int32, (half, half), 0) >= lax.broadcasted_iota(
        jnp.int32, (half, half), 1
    )
    for j in range(qfeat.shape[0]):
        f = features(query[:, j * size : (j + 1) * size], weights)
        qfeat[j] = f
        k = feat[j]
        v = jnp.concatenate([value[:, j * size : (j + 1) * size], jnp.ones((rows, size), BF16)], axis=1)
        top = jnp.where(causal, dot_nt(f[:half], k[:half]), 0.0).astype(BF16)
        left = dot_nt(f[half:], k[:half]).astype(BF16)
        right = jnp.where(causal, dot_nt(f[half:], k[half:]), 0.0).astype(BF16)
        upper = dot(top, v[:half])
        lower = dot(jnp.concatenate([left, right], axis=1), v)
        out = jnp.concatenate([upper, lower], axis=0)
        columns = slice(j * 2 * size, (j + 1) * 2 * size)

        @pl.when(block == 0)
        def _():
            result[:, columns] = out

        @pl.when(block > 0)
        def _():
            result[:, columns] = out + dot_nt(f, local[0, j])


def finish_kernel(qfeat, result, prefix, attention):
    size = attention.shape[1] // qfeat.shape[0]
    for j in range(qfeat.shape[0]):
        p = prefix[j]
        norm = p[size : size + 1].astype(F32) + p[size + 1 : size + 2].astype(F32)
        right = jnp.concatenate([p[:size], jnp.broadcast_to(norm.astype(BF16), (size, p.shape[1]))], axis=0)
        r = result[:, j * 2 * size : (j + 1) * 2 * size] + dot_nt(qfeat[j], right)
        attention[:, j * size : (j + 1) * size] = (r[:, :size] / r[:, size:]).astype(BF16)


def out_kernel(count, *refs):
    total = None
    for a, w in zip(refs[:count], refs[count : 2 * count]):
        term = dot(a[...], w[...])
        total = term if total is None else total + term
    if len(refs) == 2 * count + 2:
        total = total + refs[2 * count][...]
    refs[-1][...] = total.astype(refs[-1].dtype)


def out_product(lefts, rights, partial, dtype):
    count = len(lefts)
    rows, columns = lefts[0].shape[0], rights[0].shape[1]
    width = min(512, columns)
    specs = [pl.BlockSpec(a.shape, lambda i: (0, 0)) for a in lefts]
    specs += [pl.BlockSpec((w.shape[0], width), lambda i: (0, i)) for w in rights]
    operands = list(lefts) + list(rights)
    if partial is not None:
        specs.append(pl.BlockSpec((rows, width), lambda i: (0, i)))
        operands.append(partial)
    depth = sum(a.shape[1] for a in lefts)
    return pl.pallas_call(
        functools.partial(out_kernel, count),
        grid=(columns // width,),
        in_specs=specs,
        out_specs=pl.BlockSpec((rows, width), lambda i: (0, i)),
        out_shape=jax.ShapeDtypeStruct((rows, columns), dtype),
        compiler_params=params(32),
        cost_estimate=pl.CostEstimate(
            flops=2 * rows * columns * depth, bytes_accessed=2 * columns * depth, transcendentals=0
        ),
    )(*operands)


def swap(value, axis, bit):
    count = lax.axis_size(axis)
    return lax.ppermute(value, axis, [(i, i ^ bit) for i in range(count)])


def pack(total, size):
    high = lax.reduce_precision(total, 8, 7)
    low = total[:, size : size + 1] - high[:, size : size + 1]
    return jnp.concatenate(
        [high[:, : size + 1], low, jnp.zeros_like(total[:, : TAIL - 2])], axis=1
    ).astype(BF16)


def unpack(message, size):
    wide = message.astype(F32)
    return jnp.concatenate(
        [wide[:, :size], wide[:, size : size + 1] + wide[:, size + 1 : size + 2], jnp.zeros_like(wide[:, : TAIL - 1])],
        axis=1,
    )


def prefix(total, message, size):
    count = lax.axis_size("seq")
    mine = lax.axis_index("seq")
    side = mine % 2
    group = total.shape[0] // 2
    own = lax.dynamic_slice_in_dim(total, side * group, group, 0)
    other = lax.dynamic_slice_in_dim(message, (1 - side) * group, group, 0)
    received = unpack(swap(other, "seq", 1), size)
    pair = own + received
    earlier = jnp.zeros_like(pair)
    step = 2
    while step < count:
        sent = pack(pair + earlier, size)
        earlier = earlier + unpack(
            lax.ppermute(sent, "seq", [(i, i + step) for i in range(count - step)]), size
        )
        step *= 2
    even = side == 0
    kept = pack(earlier + jnp.where(even, 0.0, received), size)
    handed = swap(pack(earlier + jnp.where(even, own, 0.0), size), "seq", 1)
    return jnp.concatenate([jnp.where(even, kept, handed), jnp.where(even, handed, kept)], axis=0)


def shards(tokens, w_query, w_key, w_value, omega, w_out):
    rows, width = tokens.shape
    size, feats = omega.shape
    heads = w_query.shape[1] // size
    blocks = rows // BLOCK
    pairs = heads // 2
    seq_side = lax.axis_index("seq") % 2
    head_at = lax.axis_index("head")

    half = w_out.shape[0] // 2
    piece = half // 2
    w_core = swap(w_out, "head", 1)
    near, far = [], []
    for i in range(2):
        sent = lax.dynamic_slice_in_dim(w_out, seq_side * half + i * piece, piece, 0)
        near.append(swap(sent, "head", 2))
    for i in range(2):
        far.append(swap(near[i], "seq", 1))

    row_spec = pl.BlockSpec((BLOCK, width), lambda p, b: (b, 0))
    weight_spec = pl.BlockSpec((width, 2 * size), lambda p, b: (0, p))
    omega_spec = pl.BlockSpec((size, feats), lambda p, b: (0, 0))
    feat_spec = pl.BlockSpec((2, BLOCK, feats), lambda p, b: (p, b, 0))
    value_spec = pl.BlockSpec((BLOCK, 2 * size), lambda p, b: (b, p))
    state_spec = pl.BlockSpec((2, size + TAIL, feats), lambda p, b: (p, 0, 0))
    key_feat, value, total, message, local = pl.pallas_call(
        key_kernel,
        grid=(pairs, blocks),
        in_specs=[row_spec, weight_spec, weight_spec, omega_spec],
        out_specs=[
            feat_spec,
            value_spec,
            state_spec,
            state_spec,
            pl.BlockSpec((1, 2, 2 * size, feats), lambda p, b: (b, p, 0, 0)),
        ],
        out_shape=[
            jax.ShapeDtypeStruct((heads, rows, feats), BF16),
            jax.ShapeDtypeStruct((rows, heads * size), BF16),
            jax.ShapeDtypeStruct((heads, size + TAIL, feats), F32),
            jax.ShapeDtypeStruct((heads, size + TAIL, feats), BF16),
            jax.ShapeDtypeStruct((blocks, heads, 2 * size, feats), BF16),
        ],
        compiler_params=params(40),
        cost_estimate=pl.CostEstimate(
            flops=6 * 10**9, bytes_accessed=12 * 2**20, transcendentals=heads * rows * feats
        ),
        name="keys",
    )(tokens, w_key, w_value, omega)

    query_feat, result = pl.pallas_call(
        query_kernel,
        grid=(pairs, blocks),
        in_specs=[
            row_spec,
            weight_spec,
            omega_spec,
            feat_spec,
            value_spec,
            pl.BlockSpec((1, 2, 2 * size, feats), lambda p, b: (jnp.maximum(b - 1, 0), p, 0, 0)),
        ],
        out_specs=[feat_spec, pl.BlockSpec((BLOCK, 4 * size), lambda p, b: (b, p))],
        out_shape=[
            jax.ShapeDtypeStruct((heads, rows, feats), BF16),
            jax.ShapeDtypeStruct((rows, heads * 2 * size), F32),
        ],
        compiler_params=params(40),
        cost_estimate=pl.CostEstimate(
            flops=6 * 10**9, bytes_accessed=12 * 2**20, transcendentals=heads * rows * feats
        ),
        name="queries",
    )(tokens, w_query, omega, key_feat, value, local)

    earlier = prefix(total, message, size)

    attention = pl.pallas_call(
        finish_kernel,
        grid=(pairs, blocks),
        in_specs=[
            feat_spec,
            pl.BlockSpec((BLOCK, 4 * size), lambda p, b: (b, p)),
            state_spec,
        ],
        out_specs=value_spec,
        out_shape=jax.ShapeDtypeStruct((rows, heads * size), BF16),
        compiler_params=params(32),
        cost_estimate=pl.CostEstimate(
            flops=4 * rows * heads * size * feats, bytes_accessed=7 * 2**20, transcendentals=0
        ),
        name="finish",
    )(query_feat, result, earlier)

    share = rows // lax.axis_size("head")

    def part(bit):
        return lax.dynamic_slice_in_dim(attention, (head_at ^ bit) * share, share, 0)

    from_x = swap(part(2), "head", 2)
    from_diagonal = swap(swap(part(3), "head", 2), "head", 1)
    from_core = swap(part(1), "head", 1)
    near = jnp.concatenate(near, axis=0)
    far = jnp.concatenate(far, axis=0)
    core_near = swap(near, "head", 1)
    core_far = swap(far, "head", 1)

    first = out_product([part(0), from_core], [w_out, w_core], None, F32)

    def columns(value, side):
        return lax.dynamic_slice_in_dim(value, side * half, half, 1)

    return out_product(
        [
            columns(from_x, seq_side),
            columns(from_x, 1 - seq_side),
            columns(from_diagonal, seq_side),
            columns(from_diagonal, 1 - seq_side),
        ],
        [near, far, core_near, core_far],
        first,
        BF16,
    )


def solution(mesh):
    placed = (
        P("seq", None),
        P(None, "head"),
        P(None, "head"),
        P(None, "head"),
        P(),
        P("head", None),
    )
    return jax.shard_map(
        shards, mesh=mesh, in_specs=placed, out_specs=P(("seq", "head"), None), check_vma=False
    )
```

```python
import functools
import math

import jax
import jax.numpy as jnp
from jax import lax
from jax.experimental import pallas as pl
from jax.experimental.pallas import tpu as pltpu
from jax.sharding import PartitionSpec as P

BLOCK = 512
PART = 128
COST = 1000
QUAD = 4
TILE = 512
TAIL = 16
STABILIZER = 0.001
BF16 = jnp.bfloat16
F32 = jnp.float32


def params(mib):
    return pltpu.CompilerParams(vmem_limit_bytes=mib * 2**20)


def dot(a, b):
    return lax.dot_general(a, b, (((1,), (0,)), ((), ())), preferred_element_type=F32)


def dot_nt(a, b):
    return lax.dot_general(a, b, (((1,), (1,)), ((), ())), preferred_element_type=F32)


def dot_tn(a, b):
    return lax.dot_general(a, b, (((0,), (0,)), ((), ())), preferred_element_type=F32)


def halves(value):
    high = value.astype(BF16)
    return high, (value - high.astype(F32)).astype(BF16)


def feature_weights(omega):
    size, features = omega.shape
    high, low = halves(omega * size ** (-0.25))
    minus = jnp.full((2 * size, features), -1.0, BF16)
    return jnp.concatenate([high, high, low, low, minus], axis=0)


def features(rows, weights):
    size = rows.shape[1]
    high, low = halves(rows)
    square_high, square_low = halves(rows * rows * (0.5 * size ** (-0.5)))
    left = jnp.concatenate([high, low, high, low, square_high, square_low], axis=1)
    exponent = dot(left, weights)
    return ((jnp.exp(exponent) + STABILIZER) * (1.0 / math.sqrt(weights.shape[1]))).astype(BF16)


VMEM = pl.BlockSpec(memory_space=pltpu.VMEM)
SMEM = pl.BlockSpec(memory_space=pltpu.SMEM)
HBM = pl.BlockSpec(memory_space=pltpu.HBM)
ANY = pl.BlockSpec(memory_space=pl.ANY)
ROWS = 8


def narrow(state):
    size = state.shape[0] - ROWS
    norm = state[size:]
    high = norm.astype(BF16).astype(F32)
    return jnp.concatenate([state[:size], high, norm - high], axis=0).astype(BF16)


def widen(message):
    size = message.shape[0] - 2 * ROWS
    wide = message.astype(F32)
    return jnp.concatenate([wide[:size], wide[size : size + ROWS] + wide[size + ROWS :]], axis=0)


def cut_kernel(place, whole, part, sem):
    depth = part.shape[0]
    start = pl.multiple_of(place[0] * depth, depth)
    copy = pltpu.make_async_copy(whole.at[pl.ds(start, depth)], part, sem)
    copy.start()
    copy.wait()


def key_kernel(
    place, tok, wk, wv, omega, wq, wo, _, tok_out, wq_out, feat, value, own, sent_1, sent_2, sent_3, local, rest, wk_in, wv_in, om_in, keys, sem
):
    rows = tok.shape[0]
    size = omega.shape[0]
    chunk = rows // 4
    member = place[2]
    copies = []

    def fetch(source, target):
        copy = pltpu.make_async_copy(source, target, sem.at[len(copies)])
        copy.start()
        copies.append(copy)
        return copy

    def token_chunk(i):
        part = pl.ds(i * chunk, chunk)
        return fetch(tok.at[part], tok_out.at[part])

    wk_copy = fetch(wk, wk_in)
    token_copies = [token_chunk(0), token_chunk(1)]
    om_copy = fetch(omega, om_in)
    token_copies += [token_chunk(2), token_chunk(3)]
    wv_copy = fetch(wv, wv_in)
    wq_copy = fetch(wq, wq_out)
    rest_copy = fetch(wo.at[pl.ds(wo.shape[0] - rest.shape[0], rest.shape[0])], rest)

    wk_copy.wait()
    for i, copy in enumerate(token_copies):
        copy.wait()
        part = slice(i * chunk, (i + 1) * chunk)
        keys[part] = dot(tok_out[part], wk_in[...])
    wv_copy.wait()
    for start in range(0, rows, BLOCK):
        part = slice(start, start + BLOCK)
        value[part] = dot(tok_out[part], wv_in[...]).astype(BF16)
    om_copy.wait()
    weights = feature_weights(om_in[...])
    ones = jnp.ones((BLOCK, TAIL), BF16)
    heads = feat.shape[0]
    for h in range(heads):
        columns = slice(h * size, (h + 1) * size)
        for start in range(0, rows, PART):
            part = slice(start, start + PART)
            feat[h, part] = features(keys[part, columns], weights)
    for h in range(heads):
        columns = slice(h * size, (h + 1) * size)
        total = None
        for block in range(rows // BLOCK):
            part = slice(block * BLOCK, (block + 1) * BLOCK)
            if block > 0:
                norm = jnp.broadcast_to(total[size : size + 1], (size, total.shape[1]))
                local[block - 1, h] = jnp.concatenate([total[:size], norm], axis=0).astype(BF16)
            added = dot_tn(jnp.concatenate([value[part, columns], ones], axis=1), feat[h, part])[: size + ROWS]
            total = added if total is None else total + added
        group = heads // QUAD

        @pl.when(member == h // group)
        def _():
            own[h % group] = total

        @pl.when(member != h // group)
        def _():
            thin = narrow(total)
            for k, sent in ((1, sent_1), (2, sent_2), (3, sent_3)):

                @pl.when(member ^ k == h // group)
                def _():
                    sent[h % group] = thin

    wq_copy.wait()
    rest_copy.wait()


def query_kernel(first, count, tok, wq, omega, feat, value, local, *rest):
    qfeat, result, query = rest[-3:]
    rows = tok.shape[0]
    size = omega.shape[0]
    half = BLOCK // 2
    weights = feature_weights(omega[...])
    causal = lax.broadcasted_iota(jnp.int32, (half, half), 0) >= lax.broadcasted_iota(
        jnp.int32, (half, half), 1
    )
    for start in range(0, rows, BLOCK):
        part = slice(start, start + BLOCK)
        query[part] = dot(tok[part], wq[:, first * size : (first + count) * size])
    for h in range(count):
        for start in range(0, rows, PART):
            part = slice(start, start + PART)
            qfeat[h, part] = features(query[part, h * size : (h + 1) * size], weights)
    for h in range(count):
        for block in range(rows // BLOCK):
            part = slice(block * BLOCK, (block + 1) * BLOCK)
            f = qfeat[h, part]
            k = feat[first + h, part]
            v = value[part, (first + h) * size : (first + h + 1) * size]
            v = jnp.concatenate([v, jnp.ones((BLOCK, size), BF16)], axis=1)
            top = jnp.where(causal, dot_nt(f[:half], k[:half]), 0.0).astype(BF16)
            left = dot_nt(f[half:], k[:half]).astype(BF16)
            right = jnp.where(causal, dot_nt(f[half:], k[half:]), 0.0).astype(BF16)
            upper = dot(top, v[:half])
            lower = dot(jnp.concatenate([left, right], axis=1), v)
            out = jnp.concatenate([upper, lower], axis=0)
            if block > 0:
                out = out + dot_nt(f, local[block - 1, first + h])
            result[part, h * 2 * size : (h + 1) * 2 * size] = out


def group_kernel(own, one, two, three, _, sent):
    for j in range(own.shape[0]):
        sent[j] = narrow(own[j] + widen(one[j]) + widen(two[j]) + widen(three[j]))


def scan_kernel(count, message, received, *rest):
    before, (earlier, sent) = rest[:count], rest[-2:]
    for j in range(message.shape[0]):
        total = widen(received[j])
        if before:
            total = total + before[0][j]
        earlier[j] = total
        sent[j] = narrow(widen(message[j]) + total)


def last_kernel(count, place, own, one, two, three, late, *rest):
    before, outs = rest[:count], rest[-QUAD:]
    member = place[2]
    for j in range(own.shape[0]):
        total = widen(late[j])
        if before:
            total = total + before[0][j]
        states = [own[j], widen(one[j]), widen(two[j]), widen(three[j])]
        for k, out in enumerate(outs):
            value = total
            for i, state in enumerate(states):
                if i != k:
                    value = value + jnp.where((member ^ i) < (member ^ k), state, 0.0)
            out[j] = narrow(value)


def finish_kernel(bits, count, place, *refs):
    prefixes, partials, outs = refs[:QUAD], refs[QUAD:], refs[-len(bits) :]
    group = prefixes[0].shape[0]
    heads = QUAD * group
    size = outs[0].shape[1] // heads
    share = outs[0].shape[0]
    for h in range(heads):
        qfeat, result = partials[2 * (h // count)], partials[2 * (h // count) + 1]
        j = h % count
        p = prefixes[0][h % group].astype(F32)
        for k in range(1, QUAD):
            p = jnp.where(place[2] ^ k == h // group, prefixes[k][h % group].astype(F32), p)
        norm = p[size : size + 1] + p[size + ROWS : size + ROWS + 1]
        right = jnp.concatenate([p[:size], jnp.broadcast_to(norm, (size, p.shape[1]))], axis=0).astype(BF16)
        for bit, out in zip(bits, outs):
            part = pl.ds(pl.multiple_of((place[1] ^ bit) * share, share), share)
            r = result[part, j * 2 * size : (j + 1) * 2 * size] + dot_nt(qfeat[j, part, :], right)
            out[:, h * size : (h + 1) * size] = (r[:, :size] / r[:, size:]).astype(BF16)


def out_kernel(count, place, *refs):
    lefts = refs[: 2]
    rights, others = refs[2 : 2 + 2 * count], refs[2 + 2 * count :]
    streamed = len(others) > 2
    if streamed:
        before, out, tiles, sem = others
    else:
        (out,) = others
        before = None
    width = min(TILE, out.shape[1])
    copies = []
    for tile in range(out.shape[1] // width):
        here = slice(tile * width, (tile + 1) * width)
        total = before[:, here] if streamed else None
        for i, left in enumerate(lefts):
            if count == 1:
                right = rights[i][:, here]
            else:
                near, far, rest = [ref[:, here] for ref in rights[3 * i : 3 * i + 3]]
                even = place[0] == 0
                right = jnp.concatenate([jnp.where(even, near, far), jnp.where(even, far, near), rest], axis=0)
            term = dot(left[...], right)
            total = term if total is None else total + term
        if streamed:
            tiles[:, here] = total.astype(out.dtype)
            part = pl.ds(tile * width, width)
            copies.append(pltpu.make_async_copy(tiles.at[:, part], out.at[:, part], sem.at[tile]))
            copies[-1].start()
        else:
            out[:, here] = total
    for copy in copies:
        copy.wait()


def out_product(place, lefts, rights, partial, dtype):
    rows, width = lefts[0].shape[0], rights[0].shape[1]
    operands = [place] + list(lefts) + [pltpu.with_memory_space_constraint(w, pltpu.VMEM) for w in rights]
    if partial is not None:
        operands.append(partial)
    streamed = dtype == BF16
    return pl.pallas_call(
        functools.partial(out_kernel, len(rights) // 2),
        in_specs=[SMEM] + [VMEM] * (len(operands) - 1),
        out_specs=HBM if streamed else VMEM,
        out_shape=jax.ShapeDtypeStruct((rows, width), dtype) if streamed else pltpu.VMEM((rows, width), dtype),
        scratch_shapes=[pltpu.VMEM((rows, width), dtype), pltpu.SemaphoreType.DMA((width // TILE,))] if streamed else [],
        compiler_params=params(8),
        cost_estimate=pl.CostEstimate(flops=COST, bytes_accessed=COST, transcendentals=0),
        name="out",
    )(*operands)


def swap(value, axis, bit):
    count = lax.axis_size(axis)
    return lax.ppermute(value, axis, [(i, i ^ bit) for i in range(count)])


def nothing(*_):
    pass


def after(value, earlier):
    return pl.pallas_call(
        nothing,
        in_specs=[pl.BlockSpec(memory_space=pl.ANY)] * 2,
        out_specs=pl.BlockSpec(memory_space=pl.ANY),
        out_shape=jax.ShapeDtypeStruct(value.shape, value.dtype),
        input_output_aliases={0: 0},
        compiler_params=params(1),
        cost_estimate=pl.CostEstimate(flops=COST, bytes_accessed=COST, transcendentals=0),
        name="after",
    )(value, earlier)


def local_call(kernel, name, operands, specs, outs, **kwargs):
    return pl.pallas_call(
        kernel,
        in_specs=specs,
        out_specs=[VMEM] * len(outs),
        out_shape=[pltpu.VMEM(shape, dtype) for shape, dtype in outs],
        cost_estimate=pl.CostEstimate(flops=FLOPS.get(name, COST), bytes_accessed=COST, transcendentals=0),
        compiler_params=params(VMEM_MIB[name]),
        name=name,
        **kwargs,
    )(*operands)


FLOPS = dict(keys=10**10, queries=10**9)
VMEM_MIB = dict(cut=4, keys=12, queries=12, group=8, scan=8, last=8, finish=8)


def prefix(place, own, received, message, others):
    count = lax.axis_size("seq")
    wide, thin = (own.shape, F32), (message.shape, BF16)
    step = QUAD
    before = []
    while True:
        late = lax.ppermute(message, "seq", [(i, i + step) for i in range(count - step)])
        step *= 2
        if step >= count:
            break
        earlier, message = local_call(
            functools.partial(scan_kernel, len(before)),
            "scan",
            [message, late] + before,
            [VMEM] * (2 + len(before)),
            [wide, thin],
        )
        before = [earlier]
    return local_call(
        functools.partial(last_kernel, len(before)),
        "last",
        [place, own] + received + [late] + before + others,
        [SMEM] + [VMEM] * (QUAD + 1 + len(before)) + [ANY] * len(others),
        [thin] * QUAD,
    )


def shards(tokens, w_query, w_key, w_value, omega, w_out):
    rows, width = tokens.shape
    size, feats = omega.shape
    heads = w_query.shape[1] // size
    blocks = rows // BLOCK
    seq_side = lax.axis_index("seq") % 2
    head_at = lax.axis_index("head")
    place = jnp.stack([seq_side, head_at, lax.axis_index("seq") % QUAD]).astype(jnp.int32)

    depth = w_out.shape[0] * 7 // 32
    (part,) = local_call(
        cut_kernel,
        "cut",
        [place, pltpu.with_memory_space_constraint(w_out, pltpu.HBM)],
        [SMEM, HBM],
        [((depth, w_out.shape[1]), BF16)],
        scratch_shapes=[pltpu.SemaphoreType.DMA],
    )
    near_part = swap(part, "head", 2)
    w_core = swap(w_out, "head", 1)

    group = heads // QUAD
    tok, wq, key_feat, value, own, *sent, local, rest = local_call(
        key_kernel,
        "keys",
        [place] + [pltpu.with_memory_space_constraint(v, pltpu.HBM) for v in (tokens, w_key, w_value, omega, w_query, w_out)] + [part],
        [SMEM] + [HBM] * 6 + [ANY],
        [
            ((rows, width), BF16),
            (w_query.shape, BF16),
            ((heads, rows, feats), BF16),
            ((rows, heads * size), BF16),
            ((group, size + ROWS, feats), F32),
            ((group, size + 2 * ROWS, feats), BF16),
            ((group, size + 2 * ROWS, feats), BF16),
            ((group, size + 2 * ROWS, feats), BF16),
            ((max(blocks - 1, 1), heads, 2 * size, feats), BF16),
            ((w_out.shape[0] - 2 * depth, w_out.shape[1]), BF16),
        ],
        scratch_shapes=[
            pltpu.VMEM(w_key.shape, BF16),
            pltpu.VMEM(w_value.shape, BF16),
            pltpu.VMEM(omega.shape, F32),
            pltpu.VMEM((rows, heads * size), F32),
            pltpu.SemaphoreType.DMA((9,)),
        ],
    )

    count = heads // 2

    def queries(first, others):
        return local_call(
            functools.partial(query_kernel, first, count),
            "queries",
            [tok, wq, omega, key_feat, value, local] + others,
            [VMEM] * 6 + [ANY] * len(others),
            [((count, rows, feats), BF16), ((rows, count * 2 * size), F32)],
            scratch_shapes=[pltpu.VMEM((rows, count * size), F32)],
        )

    received = [swap(v, "seq", k) for k, v in enumerate(sent, 1)]
    near_rest = swap(rest, "head", 2)
    partials = queries(0, [near_part, w_core])
    (message,) = local_call(
        group_kernel, "group", [own] + received + [partials[0]], [VMEM] * QUAD + [ANY], [(sent[0].shape, BF16)]
    )
    near_part = after(near_part, message)
    core_part = swap(near_part, "head", 1)
    partials = list(partials) + list(queries(count, [message]))
    far_part = swap(near_part, "seq", 1)
    kept, *handed = prefix(place, own, received, message, [partials[2], core_part, far_part])
    prefixes = [kept] + [swap(v, "seq", k) for k, v in enumerate(handed, 1)]
    far_part = after(far_part, kept)
    core_far = swap(far_part, "head", 1)

    share = rows // lax.axis_size("head")
    bits = (2, 3, 1, 0)
    to_x, to_diagonal, to_core, mine = local_call(
        functools.partial(finish_kernel, bits, count),
        "finish",
        [place] + prefixes + partials + [near_rest, core_far],
        [SMEM] + [VMEM] * (QUAD + len(partials)) + [ANY] * 2,
        [((share, heads * size), BF16)] * len(bits),
    )
    from_x = swap(to_x, "head", 2)
    from_diagonal = swap(to_diagonal, "head", 3)
    from_core = swap(to_core, "head", 1)

    total = out_product(place, [mine, from_core], [w_out, w_core], None, F32)
    near_rest = after(near_rest, to_x)
    core_rest = swap(near_rest, "head", 1)
    rights = [near_part, far_part, near_rest, core_part, core_far, core_rest]
    return out_product(place, [from_x, from_diagonal], rights, total, BF16)


def solution(mesh):
    placed = (
        P("seq", None),
        P(None, "head"),
        P(None, "head"),
        P(None, "head"),
        P(),
        P("head", None),
    )
    return jax.shard_map(
        shards, mesh=mesh, in_specs=placed, out_specs=P(("seq", "head"), None), check_vma=False
    )
```

```python
import functools
import math

import jax
import jax.numpy as jnp
from jax import lax
from jax.experimental import pallas as pl
from jax.experimental.pallas import tpu as pltpu
from jax.sharding import PartitionSpec as P

BLOCK = 512
PART = 128
COST = 1000
QUAD = 4
TILE = 512
TAIL = 16
STABILIZER = 0.001
BF16 = jnp.bfloat16
F32 = jnp.float32


def params(mib):
    return pltpu.CompilerParams(vmem_limit_bytes=mib * 2**20)


def dot(a, b):
    return lax.dot_general(a, b, (((1,), (0,)), ((), ())), preferred_element_type=F32)


def dot_nt(a, b):
    return lax.dot_general(a, b, (((1,), (1,)), ((), ())), preferred_element_type=F32)


def dot_tn(a, b):
    return lax.dot_general(a, b, (((0,), (0,)), ((), ())), preferred_element_type=F32)


def halves(value):
    high = value.astype(BF16)
    return high, (value - high.astype(F32)).astype(BF16)


def feature_weights(omega):
    size, features = omega.shape
    high, low = halves(omega * size ** (-0.25))
    return jnp.concatenate([high, high, low, jnp.full((size, features), -1.0, BF16)], axis=0)


def features(rows, weights):
    size = rows.shape[1]
    high, low = halves(rows)
    squares = rows * rows * (0.5 * size ** (-0.5))
    squares = squares + pltpu.roll(squares, size // 2, 1)
    square_high, square_low = halves(squares)
    first = lax.broadcasted_iota(jnp.int32, rows.shape, 1) < size // 2
    square = jnp.where(first, square_high.astype(F32), square_low.astype(F32)).astype(BF16)
    exponent = dot(jnp.concatenate([high, low, high, square], axis=1), weights)
    return ((jnp.exp(exponent) + STABILIZER) * (1.0 / math.sqrt(weights.shape[1]))).astype(BF16)


VMEM = pl.BlockSpec(memory_space=pltpu.VMEM)
SMEM = pl.BlockSpec(memory_space=pltpu.SMEM)
HBM = pl.BlockSpec(memory_space=pltpu.HBM)
ANY = pl.BlockSpec(memory_space=pl.ANY)
ROWS = 8


def narrow(state):
    size = state.shape[0] - ROWS
    norm = state[size:]
    high = norm.astype(BF16).astype(F32)
    return jnp.concatenate([state[:size], high, norm - high], axis=0).astype(BF16)


def widen(message):
    size = message.shape[0] - 2 * ROWS
    wide = message.astype(F32)
    return jnp.concatenate([wide[:size], wide[size : size + ROWS] + wide[size + ROWS :]], axis=0)


def cut_kernel(place, whole, part, sem):
    depth = part.shape[0]
    start = pl.multiple_of(place[0] * depth, depth)
    copy = pltpu.make_async_copy(whole.at[pl.ds(start, depth)], part, sem)
    copy.start()
    copy.wait()


def key_kernel(
    place, tok, wk, wv, omega, wq, wo, _, tok_out, wq_out, feat, value, own, sent_1, sent_2, sent_3, local, rest, wk_in, wv_in, om_in, keys, sem
):
    rows = tok.shape[0]
    size = omega.shape[0]
    chunk = rows // 4
    member = place[2]
    copies = []

    def fetch(source, target):
        copy = pltpu.make_async_copy(source, target, sem.at[len(copies)])
        copy.start()
        copies.append(copy)
        return copy

    def token_chunk(i):
        part = pl.ds(i * chunk, chunk)
        return fetch(tok.at[part], tok_out.at[part])

    wk_copy = fetch(wk, wk_in)
    token_copies = [token_chunk(0), token_chunk(1)]
    om_copy = fetch(omega, om_in)
    token_copies += [token_chunk(2), token_chunk(3)]
    wv_copy = fetch(wv, wv_in)
    wq_copy = fetch(wq, wq_out)
    rest_copy = fetch(wo.at[pl.ds(wo.shape[0] - rest.shape[0], rest.shape[0])], rest)

    wk_copy.wait()
    for i, copy in enumerate(token_copies):
        copy.wait()
        part = slice(i * chunk, (i + 1) * chunk)
        keys[part] = dot(tok_out[part], wk_in[...])
    wv_copy.wait()
    for start in range(0, rows, BLOCK):
        part = slice(start, start + BLOCK)
        value[part] = dot(tok_out[part], wv_in[...]).astype(BF16)
    om_copy.wait()
    weights = feature_weights(om_in[...])
    ones = jnp.ones((BLOCK, TAIL), BF16)
    heads = feat.shape[0]
    for h in range(heads):
        columns = slice(h * size, (h + 1) * size)
        for start in range(0, rows, PART):
            part = slice(start, start + PART)
            feat[h, part] = features(keys[part, columns], weights)
    for h in range(heads):
        columns = slice(h * size, (h + 1) * size)
        total = None
        for block in range(rows // BLOCK):
            part = slice(block * BLOCK, (block + 1) * BLOCK)
            if block > 0:
                norm = jnp.broadcast_to(total[size : size + 1], (size, total.shape[1]))
                local[block - 1, h] = jnp.concatenate([total[:size], norm], axis=0).astype(BF16)
            added = dot_tn(jnp.concatenate([value[part, columns], ones], axis=1), feat[h, part])[: size + ROWS]
            total = added if total is None else total + added
        group = heads // QUAD

        @pl.when(member == h // group)
        def _():
            own[h % group] = total

        @pl.when(member != h // group)
        def _():
            thin = narrow(total)
            for k, sent in ((1, sent_1), (2, sent_2), (3, sent_3)):

                @pl.when(member ^ k == h // group)
                def _():
                    sent[h % group] = thin

    wq_copy.wait()
    rest_copy.wait()


def query_kernel(first, count, tok, wq, omega, feat, value, local, *rest):
    qfeat, result, query = rest[-3:]
    rows = tok.shape[0]
    size = omega.shape[0]
    half = BLOCK // 2
    weights = feature_weights(omega[...])
    causal = lax.broadcasted_iota(jnp.int32, (half, half), 0) >= lax.broadcasted_iota(
        jnp.int32, (half, half), 1
    )
    for start in range(0, rows, BLOCK):
        part = slice(start, start + BLOCK)
        query[part] = dot(tok[part], wq[:, first * size : (first + count) * size])
    for h in range(count):
        for start in range(0, rows, PART):
            part = slice(start, start + PART)
            qfeat[h, part] = features(query[part, h * size : (h + 1) * size], weights)
    for h in range(count):
        for block in range(rows // BLOCK):
            part = slice(block * BLOCK, (block + 1) * BLOCK)
            f = qfeat[h, part]
            k = feat[first + h, part]
            v = value[part, (first + h) * size : (first + h + 1) * size]
            v = jnp.concatenate([v, jnp.ones((BLOCK, size), BF16)], axis=1)
            top = jnp.where(causal, dot_nt(f[:half], k[:half]), 0.0).astype(BF16)
            left = dot_nt(f[half:], k[:half]).astype(BF16)
            right = jnp.where(causal, dot_nt(f[half:], k[half:]), 0.0).astype(BF16)
            upper = dot(top, v[:half])
            lower = dot(jnp.concatenate([left, right], axis=1), v)
            out = jnp.concatenate([upper, lower], axis=0)
            if block > 0:
                out = out + dot_nt(f, local[block - 1, first + h])
            result[part, h * 2 * size : (h + 1) * 2 * size] = out


def group_kernel(own, one, two, three, _, sent):
    for j in range(own.shape[0]):
        sent[j] = narrow(own[j] + widen(one[j]) + widen(two[j]) + widen(three[j]))


def scan_kernel(count, message, received, *rest):
    before, (earlier, sent) = rest[:count], rest[-2:]
    for j in range(message.shape[0]):
        total = widen(received[j])
        if before:
            total = total + before[0][j]
        earlier[j] = total
        sent[j] = narrow(widen(message[j]) + total)


def last_kernel(count, place, own, one, two, three, late, *rest):
    before, outs = rest[:count], rest[-QUAD:]
    member = place[2]
    for j in range(own.shape[0]):
        total = widen(late[j])
        if before:
            total = total + before[0][j]
        states = [own[j], widen(one[j]), widen(two[j]), widen(three[j])]
        for k, out in enumerate(outs):
            value = total
            for i, state in enumerate(states):
                if i != k:
                    value = value + jnp.where((member ^ i) < (member ^ k), state, 0.0)
            out[j] = narrow(value)


def finish_kernel(bits, count, place, *refs):
    prefixes, partials, outs = refs[:QUAD], refs[QUAD:], refs[-len(bits) :]
    group = prefixes[0].shape[0]
    heads = QUAD * group
    size = outs[0].shape[1] // heads
    share = outs[0].shape[0]
    for h in range(heads):
        qfeat, result = partials[2 * (h // count)], partials[2 * (h // count) + 1]
        j = h % count
        p = prefixes[0][h % group].astype(F32)
        for k in range(1, QUAD):
            p = jnp.where(place[2] ^ k == h // group, prefixes[k][h % group].astype(F32), p)
        norm = p[size : size + 1] + p[size + ROWS : size + ROWS + 1]
        right = jnp.concatenate([p[:size], jnp.broadcast_to(norm, (size, p.shape[1]))], axis=0).astype(BF16)
        for bit, out in zip(bits, outs):
            part = pl.ds(pl.multiple_of((place[1] ^ bit) * share, share), share)
            r = result[part, j * 2 * size : (j + 1) * 2 * size] + dot_nt(qfeat[j, part, :], right)
            out[:, h * size : (h + 1) * size] = (r[:, :size] / r[:, size:]).astype(BF16)


def join_kernel(place, near, far, rest, _, out):
    depth = near.shape[0]
    even = place[0] == 0
    out[:depth] = jnp.where(even, near[...], far[...])
    out[depth : 2 * depth] = jnp.where(even, far[...], near[...])
    out[2 * depth :] = rest[...]


def out_kernel(*refs):
    lefts = refs[: 2]
    rights, others = refs[2:4], refs[4:]
    streamed = len(others) > 2
    if streamed:
        before, out, tiles, sem = others
    else:
        (out,) = others
        before = None
    width = min(TILE, out.shape[1])
    copies = []
    for tile in range(out.shape[1] // width):
        here = slice(tile * width, (tile + 1) * width)
        total = before[:, here] if streamed else None
        for i, left in enumerate(lefts):
            right = rights[i][:, here]
            term = dot(left[...], right)
            total = term if total is None else total + term
        if streamed:
            tiles[:, here] = total.astype(out.dtype)
            part = pl.ds(tile * width, width)
            copies.append(pltpu.make_async_copy(tiles.at[:, part], out.at[:, part], sem.at[tile]))
            copies[-1].start()
        else:
            out[:, here] = total
    for copy in copies:
        copy.wait()


def out_product(lefts, rights, partial, dtype):
    rows, width = lefts[0].shape[0], rights[0].shape[1]
    operands = list(lefts) + [pltpu.with_memory_space_constraint(w, pltpu.VMEM) for w in rights]
    if partial is not None:
        operands.append(partial)
    streamed = dtype == BF16
    return pl.pallas_call(
        out_kernel,
        in_specs=[VMEM] * len(operands),
        out_specs=HBM if streamed else VMEM,
        out_shape=jax.ShapeDtypeStruct((rows, width), dtype) if streamed else pltpu.VMEM((rows, width), dtype),
        scratch_shapes=[pltpu.VMEM((rows, width), dtype), pltpu.SemaphoreType.DMA((width // TILE,))] if streamed else [],
        compiler_params=params(8),
        cost_estimate=pl.CostEstimate(flops=COST, bytes_accessed=COST, transcendentals=0),
        name="out",
    )(*operands)


def swap(value, axis, bit):
    count = lax.axis_size(axis)
    return lax.ppermute(value, axis, [(i, i ^ bit) for i in range(count)])


def nothing(*_):
    pass


def after(value, earlier):
    return pl.pallas_call(
        nothing,
        in_specs=[pl.BlockSpec(memory_space=pl.ANY)] * 2,
        out_specs=pl.BlockSpec(memory_space=pl.ANY),
        out_shape=jax.ShapeDtypeStruct(value.shape, value.dtype),
        input_output_aliases={0: 0},
        compiler_params=params(1),
        cost_estimate=pl.CostEstimate(flops=COST, bytes_accessed=COST, transcendentals=0),
        name="after",
    )(value, earlier)


def local_call(kernel, name, operands, specs, outs, **kwargs):
    return pl.pallas_call(
        kernel,
        in_specs=specs,
        out_specs=[VMEM] * len(outs),
        out_shape=[pltpu.VMEM(shape, dtype) for shape, dtype in outs],
        cost_estimate=pl.CostEstimate(flops=FLOPS.get(name, COST), bytes_accessed=COST, transcendentals=0),
        compiler_params=params(VMEM_MIB[name]),
        name=name,
        **kwargs,
    )(*operands)


FLOPS = dict(keys=10**10, queries=3 * 10**8)
VMEM_MIB = dict(join=4, cut=4, keys=12, queries=12, group=8, scan=8, last=8, finish=8)


def prefix(place, own, received, message, others):
    count = lax.axis_size("seq")
    wide, thin = (own.shape, F32), (message.shape, BF16)
    step = QUAD
    before = []
    while True:
        late = lax.ppermute(message, "seq", [(i, i + step) for i in range(count - step)])
        step *= 2
        if step >= count:
            break
        earlier, message = local_call(
            functools.partial(scan_kernel, len(before)),
            "scan",
            [message, late] + before,
            [VMEM] * (2 + len(before)),
            [wide, thin],
        )
        before = [earlier]
    return local_call(
        functools.partial(last_kernel, len(before)),
        "last",
        [place, own] + received + [late] + before + others,
        [SMEM] + [VMEM] * (QUAD + 1 + len(before)) + [ANY] * len(others),
        [thin] * QUAD,
    )


def shards(tokens, w_query, w_key, w_value, omega, w_out):
    rows, width = tokens.shape
    size, feats = omega.shape
    heads = w_query.shape[1] // size
    blocks = rows // BLOCK
    seq_side = lax.axis_index("seq") % 2
    head_at = lax.axis_index("head")
    place = jnp.stack([seq_side, head_at, lax.axis_index("seq") % QUAD]).astype(jnp.int32)

    depth = w_out.shape[0] // 4
    (part,) = local_call(
        cut_kernel,
        "cut",
        [place, pltpu.with_memory_space_constraint(w_out, pltpu.HBM)],
        [SMEM, HBM],
        [((depth, w_out.shape[1]), BF16)],
        scratch_shapes=[pltpu.SemaphoreType.DMA],
    )
    near_part = swap(part, "head", 2)
    w_core = swap(w_out, "head", 1)

    group = heads // QUAD
    tok, wq, key_feat, value, own, *sent, local, rest = local_call(
        key_kernel,
        "keys",
        [place] + [pltpu.with_memory_space_constraint(v, pltpu.HBM) for v in (tokens, w_key, w_value, omega, w_query, w_out)] + [part],
        [SMEM] + [HBM] * 6 + [ANY],
        [
            ((rows, width), BF16),
            (w_query.shape, BF16),
            ((heads, rows, feats), BF16),
            ((rows, heads * size), BF16),
            ((group, size + ROWS, feats), F32),
            ((group, size + 2 * ROWS, feats), BF16),
            ((group, size + 2 * ROWS, feats), BF16),
            ((group, size + 2 * ROWS, feats), BF16),
            ((max(blocks - 1, 1), heads, 2 * size, feats), BF16),
            ((w_out.shape[0] - 2 * depth, w_out.shape[1]), BF16),
        ],
        scratch_shapes=[
            pltpu.VMEM(w_key.shape, BF16),
            pltpu.VMEM(w_value.shape, BF16),
            pltpu.VMEM(omega.shape, F32),
            pltpu.VMEM((rows, heads * size), F32),
            pltpu.SemaphoreType.DMA((9,)),
        ],
    )

    count = heads // 2

    def queries(first, others):
        return local_call(
            functools.partial(query_kernel, first, count),
            "queries",
            [tok, wq, omega, key_feat, value, local] + others,
            [VMEM] * 6 + [ANY] * len(others),
            [((count, rows, feats), BF16), ((rows, count * 2 * size), F32)],
            scratch_shapes=[pltpu.VMEM((rows, count * size), F32)],
        )

    received = [swap(v, "seq", k) for k, v in enumerate(sent, 1)]
    near_rest = swap(rest, "head", 2)
    partials = queries(0, [near_part, w_core])
    (message,) = local_call(
        group_kernel, "group", [own] + received + [partials[0]], [VMEM] * QUAD + [ANY], [(sent[0].shape, BF16)]
    )
    near_part = after(near_part, message)
    partials = list(partials) + list(queries(count, [message]))
    far_part = swap(near_part, "seq", 1)
    kept, *handed = prefix(place, own, received, message, [partials[2]])
    prefixes = [kept] + [swap(v, "seq", k) for k, v in enumerate(handed, 1)]
    share = rows // lax.axis_size("head")
    bits = (2, 3, 1, 0)
    to_x, to_diagonal, to_core, mine = local_call(
        functools.partial(finish_kernel, bits, count),
        "finish",
        [place] + prefixes + partials + [near_rest, far_part],
        [SMEM] + [VMEM] * (QUAD + len(partials)) + [ANY] * 2,
        [((share, heads * size), BF16)] * len(bits),
    )
    from_x = swap(to_x, "head", 2)
    from_diagonal = swap(to_diagonal, "head", 3)
    from_core = swap(to_core, "head", 1)

    total = out_product([mine, from_core], [w_out, w_core], None, F32)
    (w_across,) = local_call(
        join_kernel,
        "join",
        [place, near_part, far_part, near_rest, to_x],
        [SMEM] + [VMEM] * 3 + [ANY],
        [(w_out.shape, BF16)],
    )
    w_diagonal = swap(w_across, "head", 1)
    return out_product([from_x, from_diagonal], [w_across, w_diagonal], total, BF16)


def solution(mesh):
    placed = (
        P("seq", None),
        P(None, "head"),
        P(None, "head"),
        P(None, "head"),
        P(),
        P("head", None),
    )
    return jax.shard_map(
        shards, mesh=mesh, in_specs=placed, out_specs=P(("seq", "head"), None), check_vma=False
    )
```

```python
import functools
import math

import jax
import jax.numpy as jnp
from jax import lax
from jax.experimental import pallas as pl
from jax.experimental.pallas import tpu as pltpu
from jax.sharding import PartitionSpec as P

BLOCK = 512
PART = 128
COST = 1000
QUAD = 4
TILE = 512
TAIL = 16
STABILIZER = 0.001
BF16 = jnp.bfloat16
F32 = jnp.float32


def params(mib):
    return pltpu.CompilerParams(vmem_limit_bytes=mib * 2**20)


def dot(a, b):
    return lax.dot_general(a, b, (((1,), (0,)), ((), ())), preferred_element_type=F32)


def dot_nt(a, b):
    return lax.dot_general(a, b, (((1,), (1,)), ((), ())), preferred_element_type=F32)


def dot_tn(a, b):
    return lax.dot_general(a, b, (((0,), (0,)), ((), ())), preferred_element_type=F32)


def halves(value):
    high = value.astype(BF16)
    return high, (value - high.astype(F32)).astype(BF16)


def feature_weights(omega):
    size, features = omega.shape
    high, low = halves(omega * size ** (-0.25))
    return jnp.concatenate([high, high, low, jnp.full((size, features), -1.0, BF16)], axis=0)


def features(rows, weights):
    size = rows.shape[1]
    high, low = halves(rows)
    squares = rows * rows * (0.5 * size ** (-0.5))
    squares = squares + pltpu.roll(squares, size // 2, 1)
    square_high, square_low = halves(squares)
    first = lax.broadcasted_iota(jnp.int32, rows.shape, 1) < size // 2
    square = jnp.where(first, square_high.astype(F32), square_low.astype(F32)).astype(BF16)
    exponent = dot(jnp.concatenate([high, low, high, square], axis=1), weights)
    return ((jnp.exp(exponent) + STABILIZER) * (1.0 / math.sqrt(weights.shape[1]))).astype(BF16)


VMEM = pl.BlockSpec(memory_space=pltpu.VMEM)
SMEM = pl.BlockSpec(memory_space=pltpu.SMEM)
HBM = pl.BlockSpec(memory_space=pltpu.HBM)
ANY = pl.BlockSpec(memory_space=pl.ANY)
ROWS = 8


def narrow(state):
    size = state.shape[0] - ROWS
    norm = state[size:]
    high = norm.astype(BF16).astype(F32)
    return jnp.concatenate([state[:size], high, norm - high], axis=0).astype(BF16)


def widen(message):
    size = message.shape[0] - 2 * ROWS
    wide = message.astype(F32)
    return jnp.concatenate([wide[:size], wide[size : size + ROWS] + wide[size + ROWS :]], axis=0)


def cut_kernel(place, whole, part, sem):
    depth = part.shape[0]
    start = pl.multiple_of(place[0] * depth, depth)
    copy = pltpu.make_async_copy(whole.at[pl.ds(start, depth)], part, sem)
    copy.start()
    copy.wait()


def key_kernel(
    place, tok, wk, wv, omega, wq, wo, _, tok_out, wq_out, feat, value, own, sent_1, sent_2, sent_3, local, rest, wv_in, om_in, keys, sem
):
    rows = tok.shape[0]
    size = omega.shape[0]
    chunk = rows // 4
    member = place[2]
    copies = []

    def fetch(source, target):
        copy = pltpu.make_async_copy(source, target, sem.at[len(copies)])
        copy.start()
        copies.append(copy)
        return copy

    def token_chunk(i):
        part = pl.ds(i * chunk, chunk)
        return fetch(tok.at[part], tok_out.at[part])

    token_copies = [token_chunk(0), token_chunk(1)]
    om_copy = fetch(omega, om_in)
    token_copies += [token_chunk(2), token_chunk(3)]
    wv_copy = fetch(wv, wv_in)
    wq_copy = fetch(wq, wq_out)
    rest_copy = fetch(wo.at[pl.ds(wo.shape[0] - rest.shape[0], rest.shape[0])], rest)

    for i, copy in enumerate(token_copies):
        copy.wait()
        part = slice(i * chunk, (i + 1) * chunk)
        keys[part] = dot(tok_out[part], wk[...])
    wv_copy.wait()
    for start in range(0, rows, BLOCK):
        part = slice(start, start + BLOCK)
        value[part] = dot(tok_out[part], wv_in[...]).astype(BF16)
    om_copy.wait()
    weights = feature_weights(om_in[...])
    ones = jnp.ones((BLOCK, TAIL), BF16)
    heads = feat.shape[0]
    for h in range(heads):
        columns = slice(h * size, (h + 1) * size)
        for start in range(0, rows, PART):
            part = slice(start, start + PART)
            feat[h, part] = features(keys[part, columns], weights)
    for h in range(heads):
        columns = slice(h * size, (h + 1) * size)
        total = None
        for block in range(rows // BLOCK):
            part = slice(block * BLOCK, (block + 1) * BLOCK)
            if block > 0:
                norm = jnp.broadcast_to(total[size : size + 1], (size, total.shape[1]))
                local[block - 1, h] = jnp.concatenate([total[:size], norm], axis=0).astype(BF16)
            added = dot_tn(jnp.concatenate([value[part, columns], ones], axis=1), feat[h, part])[: size + ROWS]
            total = added if total is None else total + added
        group = heads // QUAD

        @pl.when(member == h // group)
        def _():
            own[h % group] = total

        @pl.when(member != h // group)
        def _():
            thin = narrow(total)
            for k, sent in ((1, sent_1), (2, sent_2), (3, sent_3)):

                @pl.when(member ^ k == h // group)
                def _():
                    sent[h % group] = thin

    wq_copy.wait()
    rest_copy.wait()


def query_kernel(first, count, tok, wq, omega, feat, value, local, *rest):
    qfeat, result, query = rest[-3:]
    rows = tok.shape[0]
    size = omega.shape[0]
    half = BLOCK // 2
    weights = feature_weights(omega[...])
    causal = lax.broadcasted_iota(jnp.int32, (half, half), 0) >= lax.broadcasted_iota(
        jnp.int32, (half, half), 1
    )
    for start in range(0, rows, BLOCK):
        part = slice(start, start + BLOCK)
        query[part] = dot(tok[part], wq[:, first * size : (first + count) * size])
    for h in range(count):
        for start in range(0, rows, PART):
            part = slice(start, start + PART)
            qfeat[h, part] = features(query[part, h * size : (h + 1) * size], weights)
    for h in range(count):
        for block in range(rows // BLOCK):
            part = slice(block * BLOCK, (block + 1) * BLOCK)
            f = qfeat[h, part]
            k = feat[first + h, part]
            v = value[part, (first + h) * size : (first + h + 1) * size]
            v = jnp.concatenate([v, jnp.ones((BLOCK, size), BF16)], axis=1)
            top = jnp.where(causal, dot_nt(f[:half], k[:half]), 0.0).astype(BF16)
            left = dot_nt(f[half:], k[:half]).astype(BF16)
            right = jnp.where(causal, dot_nt(f[half:], k[half:]), 0.0).astype(BF16)
            upper = dot(top, v[:half])
            lower = dot(jnp.concatenate([left, right], axis=1), v)
            out = jnp.concatenate([upper, lower], axis=0)
            if block > 0:
                out = out + dot_nt(f, local[block - 1, first + h])
            result[part, h * 2 * size : (h + 1) * 2 * size] = out


def group_kernel(own, one, two, three, _, _2, sent):
    for j in range(own.shape[0]):
        sent[j] = narrow(own[j] + widen(one[j]) + widen(two[j]) + widen(three[j]))


def scan_kernel(count, message, received, *rest):
    before, (earlier, sent) = rest[:count], rest[-2:]
    for j in range(message.shape[0]):
        total = widen(received[j])
        if before:
            total = total + before[0][j]
        earlier[j] = total
        sent[j] = narrow(widen(message[j]) + total)


def last_kernel(count, place, own, one, two, three, late, *rest):
    before, outs = rest[:count], rest[-QUAD:]
    member = place[2]
    for j in range(own.shape[0]):
        total = widen(late[j])
        if before:
            total = total + before[0][j]
        states = [own[j], widen(one[j]), widen(two[j]), widen(three[j])]
        for k, out in enumerate(outs):
            value = total
            for i, state in enumerate(states):
                if i != k:
                    value = value + jnp.where((member ^ i) < (member ^ k), state, 0.0)
            out[j] = narrow(value)


def finish_kernel(bits, count, place, *refs):
    prefixes, partials, outs = refs[:QUAD], refs[QUAD:], refs[-len(bits) :]
    group = prefixes[0].shape[0]
    heads = QUAD * group
    size = outs[0].shape[1] // heads
    share = outs[0].shape[0]
    for h in range(heads):
        qfeat, result = partials[2 * (h // count)], partials[2 * (h // count) + 1]
        j = h % count
        p = prefixes[0][h % group].astype(F32)
        for k in range(1, QUAD):
            p = jnp.where(place[2] ^ k == h // group, prefixes[k][h % group].astype(F32), p)
        norm = p[size : size + 1] + p[size + ROWS : size + ROWS + 1]
        right = jnp.concatenate([p[:size], jnp.broadcast_to(norm, (size, p.shape[1]))], axis=0).astype(BF16)
        for bit, out in zip(bits, outs):
            part = pl.ds(pl.multiple_of((place[1] ^ bit) * share, share), share)
            r = result[part, j * 2 * size : (j + 1) * 2 * size] + dot_nt(qfeat[j, part, :], right)
            out[:, h * size : (h + 1) * size] = (r[:, :size] / r[:, size:]).astype(BF16)


def join_kernel(place, near, far, out):
    depth = near.shape[0]
    even = place[0] == 0
    out[:depth] = jnp.where(even, near[...], far[...])
    out[depth:] = jnp.where(even, far[...], near[...])


def out_kernel(count, *refs):
    lefts, rights, others = refs[:2], refs[2 : 2 + 2 * count], refs[2 + 2 * count :]
    streamed = len(others) > 2
    if streamed:
        before, out, tiles, sem = others
    else:
        (out,) = others
        before = None
    width = min(TILE, out.shape[1])
    copies = []
    for tile in range(out.shape[1] // width):
        here = slice(tile * width, (tile + 1) * width)
        total = before[:, here] if streamed else None
        for i, left in enumerate(lefts):
            parts = [ref[:, here] for ref in rights[count * i : count * (i + 1)]]
            term = dot(left[...], jnp.concatenate(parts, axis=0) if count > 1 else parts[0])
            total = term if total is None else total + term
        if streamed:
            tiles[:, here] = total.astype(out.dtype)
            part = pl.ds(tile * width, width)
            copies.append(pltpu.make_async_copy(tiles.at[:, part], out.at[:, part], sem.at[tile]))
            copies[-1].start()
        else:
            out[:, here] = total
    for copy in copies:
        copy.wait()


def out_product(lefts, rights, partial, dtype):
    rows, width = lefts[0].shape[0], rights[0][0].shape[1]
    operands = list(lefts) + [pltpu.with_memory_space_constraint(w, pltpu.VMEM) for group in rights for w in group]
    if partial is not None:
        operands.append(partial)
    streamed = dtype == BF16
    return pl.pallas_call(
        functools.partial(out_kernel, len(rights[0])),
        in_specs=[VMEM] * len(operands),
        out_specs=HBM if streamed else VMEM,
        out_shape=jax.ShapeDtypeStruct((rows, width), dtype) if streamed else pltpu.VMEM((rows, width), dtype),
        scratch_shapes=[pltpu.VMEM((rows, width), dtype), pltpu.SemaphoreType.DMA((width // TILE,))] if streamed else [],
        compiler_params=params(8),
        cost_estimate=pl.CostEstimate(flops=COST, bytes_accessed=COST, transcendentals=0),
        name="out",
    )(*operands)


def swap(value, axis, bit):
    count = lax.axis_size(axis)
    return lax.ppermute(value, axis, [(i, i ^ bit) for i in range(count)])


def nothing(*_):
    pass


def after(value, earlier):
    return pl.pallas_call(
        nothing,
        in_specs=[pl.BlockSpec(memory_space=pl.ANY)] * 2,
        out_specs=pl.BlockSpec(memory_space=pl.ANY),
        out_shape=jax.ShapeDtypeStruct(value.shape, value.dtype),
        input_output_aliases={0: 0},
        compiler_params=params(1),
        cost_estimate=pl.CostEstimate(flops=COST, bytes_accessed=COST, transcendentals=0),
        name="after",
    )(value, earlier)


def local_call(kernel, name, operands, specs, outs, **kwargs):
    return pl.pallas_call(
        kernel,
        in_specs=specs,
        out_specs=[VMEM] * len(outs),
        out_shape=[pltpu.VMEM(shape, dtype) for shape, dtype in outs],
        cost_estimate=pl.CostEstimate(flops=FLOPS.get(name, COST), bytes_accessed=COST, transcendentals=0),
        compiler_params=params(VMEM_MIB[name]),
        name=name,
        **kwargs,
    )(*operands)


FLOPS = dict(keys=10**10, queries=3 * 10**8)
VMEM_MIB = dict(join=4, cut=4, keys=12, queries=12, group=8, scan=8, last=8, finish=8)


def prefix(place, own, received, message, others):
    count = lax.axis_size("seq")
    wide, thin = (own.shape, F32), (message.shape, BF16)
    step = QUAD
    before = []
    while True:
        late = lax.ppermute(message, "seq", [(i, i + step) for i in range(count - step)])
        step *= 2
        if step >= count:
            break
        earlier, message = local_call(
            functools.partial(scan_kernel, len(before)),
            "scan",
            [message, late] + before,
            [VMEM] * (2 + len(before)),
            [wide, thin],
        )
        before = [earlier]
    return local_call(
        functools.partial(last_kernel, len(before)),
        "last",
        [place, own] + received + [late] + before + others,
        [SMEM] + [VMEM] * (QUAD + 1 + len(before)) + [ANY] * len(others),
        [thin] * QUAD,
    )


def shards(tokens, w_query, w_key, w_value, omega, w_out):
    rows, width = tokens.shape
    size, feats = omega.shape
    heads = w_query.shape[1] // size
    blocks = rows // BLOCK
    seq_side = lax.axis_index("seq") % 2
    head_at = lax.axis_index("head")
    place = jnp.stack([seq_side, head_at, lax.axis_index("seq") % QUAD]).astype(jnp.int32)

    depth = w_out.shape[0] // 4
    (part,) = local_call(
        cut_kernel,
        "cut",
        [place, pltpu.with_memory_space_constraint(w_out, pltpu.HBM)],
        [SMEM, HBM],
        [((depth, w_out.shape[1]), BF16)],
        scratch_shapes=[pltpu.SemaphoreType.DMA],
    )
    near_part = swap(part, "head", 2)
    w_core = swap(w_out, "head", 1)

    group = heads // QUAD
    tok, wq, key_feat, value, own, *sent, local, rest = local_call(
        key_kernel,
        "keys",
        [place, pltpu.with_memory_space_constraint(tokens, pltpu.HBM), pltpu.with_memory_space_constraint(w_key, pltpu.VMEM)]
        + [pltpu.with_memory_space_constraint(v, pltpu.HBM) for v in (w_value, omega, w_query, w_out)]
        + [part],
        [SMEM, HBM, VMEM] + [HBM] * 4 + [ANY],
        [
            ((rows, width), BF16),
            (w_query.shape, BF16),
            ((heads, rows, feats), BF16),
            ((rows, heads * size), BF16),
            ((group, size + ROWS, feats), F32),
            ((group, size + 2 * ROWS, feats), BF16),
            ((group, size + 2 * ROWS, feats), BF16),
            ((group, size + 2 * ROWS, feats), BF16),
            ((max(blocks - 1, 1), heads, 2 * size, feats), BF16),
            ((w_out.shape[0] - 2 * depth, w_out.shape[1]), BF16),
        ],
        scratch_shapes=[
            pltpu.VMEM(w_value.shape, BF16),
            pltpu.VMEM(omega.shape, F32),
            pltpu.VMEM((rows, heads * size), F32),
            pltpu.SemaphoreType.DMA((9,)),
        ],
    )

    count = heads // 2

    def queries(first, others):
        return local_call(
            functools.partial(query_kernel, first, count),
            "queries",
            [tok, wq, omega, key_feat, value, local] + others,
            [VMEM] * 6 + [ANY] * len(others),
            [((count, rows, feats), BF16), ((rows, count * 2 * size), F32)],
            scratch_shapes=[pltpu.VMEM((rows, count * size), F32)],
        )

    received = [swap(v, "seq", k) for k, v in enumerate(sent, 1)]
    near_rest = swap(rest, "head", 2)
    partials = queries(0, [w_core])
    (message,) = local_call(
        group_kernel, "group", [own] + received + [partials[0], near_part], [VMEM] * QUAD + [ANY] * 2, [(sent[0].shape, BF16)]
    )
    near_part = after(near_part, message)
    partials = list(partials) + list(queries(count, [message]))
    far_part = swap(near_part, "seq", 1)
    kept, *handed = prefix(place, own, received, message, [partials[2]])
    prefixes = [kept] + [swap(v, "seq", k) for k, v in enumerate(handed, 1)]
    (joined,) = local_call(
        join_kernel,
        "join",
        [place, near_part, far_part],
        [SMEM] + [VMEM] * 2,
        [((2 * depth, w_out.shape[1]), BF16)],
    )

    share = rows // lax.axis_size("head")
    bits = (2, 3, 1, 0)
    to_x, to_diagonal, to_core, mine = local_call(
        functools.partial(finish_kernel, bits, count),
        "finish",
        [place] + prefixes + partials + [near_rest, joined],
        [SMEM] + [VMEM] * (QUAD + len(partials)) + [ANY] * 2,
        [((share, heads * size), BF16)] * len(bits),
    )
    from_x = swap(to_x, "head", 2)
    from_diagonal = swap(to_diagonal, "head", 3)
    from_core = swap(to_core, "head", 1)

    total = out_product([mine, from_core], [[w_out], [w_core]], None, F32)
    pieces = [after(v, to_x) for v in (joined, near_rest)]
    core_pieces = [swap(v, "head", 1) for v in pieces]
    return out_product([from_x, from_diagonal], [pieces, core_pieces], total, BF16)


def solution(mesh):
    placed = (
        P("seq", None),
        P(None, "head"),
        P(None, "head"),
        P(None, "head"),
        P(),
        P("head", None),
    )
    return jax.shard_map(
        shards, mesh=mesh, in_specs=placed, out_specs=P(("seq", "head"), None), check_vma=False
    )
```

```python
import functools
import math

import jax
import jax.numpy as jnp
from jax import lax
from jax.experimental import pallas as pl
from jax.experimental.pallas import tpu as pltpu
from jax.sharding import PartitionSpec as P

BLOCK = 512
PART = 128
COST = 1000
QUAD = 4
TILE = 512
TAIL = 16
STABILIZER = 0.001
BF16 = jnp.bfloat16
F32 = jnp.float32


def params(mib):
    return pltpu.CompilerParams(vmem_limit_bytes=mib * 2**20)


def dot(a, b):
    return lax.dot_general(a, b, (((1,), (0,)), ((), ())), preferred_element_type=F32)


def dot_nt(a, b):
    return lax.dot_general(a, b, (((1,), (1,)), ((), ())), preferred_element_type=F32)


def dot_tn(a, b):
    return lax.dot_general(a, b, (((0,), (0,)), ((), ())), preferred_element_type=F32)


def halves(value):
    high = value.astype(BF16)
    return high, (value - high.astype(F32)).astype(BF16)


def feature_weights(omega):
    size, features = omega.shape
    high, low = halves(omega * size ** (-0.25))
    return jnp.concatenate([high, high, low, jnp.full((size, features), -1.0, BF16)], axis=0)


def features(rows, weights):
    size = rows.shape[1]
    high, low = halves(rows)
    squares = rows * rows * (0.5 * size ** (-0.5))
    squares = squares + pltpu.roll(squares, size // 2, 1)
    square_high, square_low = halves(squares)
    first = lax.broadcasted_iota(jnp.int32, rows.shape, 1) < size // 2
    square = jnp.where(first, square_high.astype(F32), square_low.astype(F32)).astype(BF16)
    exponent = dot(jnp.concatenate([high, low, high, square], axis=1), weights)
    return ((jnp.exp(exponent) + STABILIZER) * (1.0 / math.sqrt(weights.shape[1]))).astype(BF16)


VMEM = pl.BlockSpec(memory_space=pltpu.VMEM)
SMEM = pl.BlockSpec(memory_space=pltpu.SMEM)
HBM = pl.BlockSpec(memory_space=pltpu.HBM)
ANY = pl.BlockSpec(memory_space=pl.ANY)
ROWS = 8


def narrow(state):
    size = state.shape[0] - ROWS
    norm = state[size:]
    high = norm.astype(BF16).astype(F32)
    return jnp.concatenate([state[:size], high, norm - high], axis=0).astype(BF16)


def widen(message):
    size = message.shape[0] - 2 * ROWS
    wide = message.astype(F32)
    return jnp.concatenate([wide[:size], wide[size : size + ROWS] + wide[size + ROWS :]], axis=0)


def cut_kernel(place, whole, part, sem):
    depth = part.shape[0]
    start = pl.multiple_of(place[0] * depth, depth)
    copy = pltpu.make_async_copy(whole.at[pl.ds(start, depth)], part, sem)
    copy.start()
    copy.wait()


def key_kernel(
    place, tok, wk, wv, omega, wq, wo, _, tok_out, wq_out, feat, value, own, sent_1, sent_2, sent_3, local, rest, wv_in, om_in, keys, sem
):
    rows = tok.shape[0]
    size = omega.shape[0]
    chunk = rows // 4
    member = place[2]
    copies = []

    def fetch(source, target):
        copy = pltpu.make_async_copy(source, target, sem.at[len(copies)])
        copy.start()
        copies.append(copy)
        return copy

    def token_chunk(i):
        part = pl.ds(i * chunk, chunk)
        return fetch(tok.at[part], tok_out.at[part])

    token_copies = [token_chunk(0), token_chunk(1)]
    om_copy = fetch(omega, om_in)
    token_copies += [token_chunk(2), token_chunk(3)]
    wv_copy = fetch(wv, wv_in)
    wq_copy = fetch(wq, wq_out)
    rest_copy = fetch(wo.at[pl.ds(wo.shape[0] - rest.shape[0], rest.shape[0])], rest)

    for i, copy in enumerate(token_copies):
        copy.wait()
        part = slice(i * chunk, (i + 1) * chunk)
        keys[part] = dot(tok_out[part], wk[...])
    wv_copy.wait()
    for start in range(0, rows, BLOCK):
        part = slice(start, start + BLOCK)
        value[part] = dot(tok_out[part], wv_in[...]).astype(BF16)
    om_copy.wait()
    weights = feature_weights(om_in[...])
    ones = jnp.ones((BLOCK, TAIL), BF16)
    heads = feat.shape[0]
    for h in range(heads):
        columns = slice(h * size, (h + 1) * size)
        for start in range(0, rows, PART):
            part = slice(start, start + PART)
            feat[h, part] = features(keys[part, columns], weights)
    for h in range(heads):
        columns = slice(h * size, (h + 1) * size)
        total = None
        for block in range(rows // BLOCK):
            part = slice(block * BLOCK, (block + 1) * BLOCK)
            if block > 0:
                norm = jnp.broadcast_to(total[size : size + 1], (size, total.shape[1]))
                local[block - 1, h] = jnp.concatenate([total[:size], norm], axis=0).astype(BF16)
            added = dot_tn(jnp.concatenate([value[part, columns], ones], axis=1), feat[h, part])[: size + ROWS]
            total = added if total is None else total + added
        group = heads // QUAD

        @pl.when(member == h // group)
        def _():
            own[h % group] = total

        @pl.when(member != h // group)
        def _():
            thin = narrow(total)
            for k, sent in ((1, sent_1), (2, sent_2), (3, sent_3)):

                @pl.when(member ^ k == h // group)
                def _():
                    sent[h % group] = thin

    wq_copy.wait()
    rest_copy.wait()


def query_kernel(first, count, tok, wq, omega, feat, value, local, *rest):
    qfeat, result, query = rest[-3:]
    rows = tok.shape[0]
    size = omega.shape[0]
    half = BLOCK // 2
    weights = feature_weights(omega[...])
    causal = lax.broadcasted_iota(jnp.int32, (half, half), 0) >= lax.broadcasted_iota(
        jnp.int32, (half, half), 1
    )
    for start in range(0, rows, BLOCK):
        part = slice(start, start + BLOCK)
        query[part] = dot(tok[part], wq[:, first * size : (first + count) * size])
    for h in range(count):
        for start in range(0, rows, PART):
            part = slice(start, start + PART)
            qfeat[h, part] = features(query[part, h * size : (h + 1) * size], weights)
    for h in range(count):
        for block in range(rows // BLOCK):
            part = slice(block * BLOCK, (block + 1) * BLOCK)
            f = qfeat[h, part]
            k = feat[first + h, part]
            v = value[part, (first + h) * size : (first + h + 1) * size]
            v = jnp.concatenate([v, jnp.ones((BLOCK, size), BF16)], axis=1)
            top = jnp.where(causal, dot_nt(f[:half], k[:half]), 0.0).astype(BF16)
            left = dot_nt(f[half:], k[:half]).astype(BF16)
            right = jnp.where(causal, dot_nt(f[half:], k[half:]), 0.0).astype(BF16)
            upper = dot(top, v[:half])
            lower = dot(jnp.concatenate([left, right], axis=1), v)
            out = jnp.concatenate([upper, lower], axis=0)
            if block > 0:
                out = out + dot_nt(f, local[block - 1, first + h])
            result[part, h * 2 * size : (h + 1) * 2 * size] = out


def group_kernel(own, one, two, three, _, _2, sent):
    for j in range(own.shape[0]):
        sent[j] = narrow(own[j] + widen(one[j]) + widen(two[j]) + widen(three[j]))


def scan_kernel(count, message, received, *rest):
    before, (earlier, sent) = rest[:count], rest[-2:]
    for j in range(message.shape[0]):
        total = widen(received[j])
        if before:
            total = total + before[0][j]
        earlier[j] = total
        sent[j] = narrow(widen(message[j]) + total)


def last_kernel(count, place, own, one, two, three, late, *rest):
    before, outs = rest[:count], rest[-QUAD:]
    member = place[2]
    for j in range(own.shape[0]):
        total = widen(late[j])
        if before:
            total = total + before[0][j]
        states = [own[j], widen(one[j]), widen(two[j]), widen(three[j])]
        for k, out in enumerate(outs):
            value = total
            for i, state in enumerate(states):
                if i != k:
                    value = value + jnp.where((member ^ i) < (member ^ k), state, 0.0)
            out[j] = narrow(value)


def finish_kernel(bits, count, place, *refs):
    prefixes, partials, outs = refs[:QUAD], refs[QUAD:], refs[-len(bits) :]
    group = prefixes[0].shape[0]
    heads = QUAD * group
    size = outs[0].shape[1] // heads
    share = outs[0].shape[0]
    for h in range(heads):
        qfeat, result = partials[2 * (h // count)], partials[2 * (h // count) + 1]
        j = h % count
        p = prefixes[0][h % group].astype(F32)
        for k in range(1, QUAD):
            p = jnp.where(place[2] ^ k == h // group, prefixes[k][h % group].astype(F32), p)
        norm = p[size : size + 1] + p[size + ROWS : size + ROWS + 1]
        right = jnp.concatenate([p[:size], jnp.broadcast_to(norm, (size, p.shape[1]))], axis=0).astype(BF16)
        for bit, out in zip(bits, outs):
            part = pl.ds(pl.multiple_of((place[1] ^ bit) * share, share), share)
            r = result[part, j * 2 * size : (j + 1) * 2 * size] + dot_nt(qfeat[j, part, :], right)
            out[:, h * size : (h + 1) * size] = (r[:, :size] / r[:, size:]).astype(BF16)


def join_kernel(place, near, far, out):
    depth = near.shape[0]
    even = place[0] == 0
    out[:depth] = jnp.where(even, near[...], far[...])
    out[depth:] = jnp.where(even, far[...], near[...])


def out_kernel(count, *refs):
    lefts, rights, others = refs[:2], refs[2 : 2 + 2 * count], refs[2 + 2 * count :]
    streamed = len(others) > 2
    if streamed:
        before, out, tiles, sem = others
    else:
        (out,) = others
        before = None
    width = min(TILE, out.shape[1])
    copies = []
    for tile in range(out.shape[1] // width):
        here = slice(tile * width, (tile + 1) * width)
        total = before[:, here] if streamed else None
        for i, left in enumerate(lefts):
            parts = [ref[:, here] for ref in rights[count * i : count * (i + 1)]]
            term = dot(left[...], jnp.concatenate(parts, axis=0) if count > 1 else parts[0])
            total = term if total is None else total + term
        if streamed:
            tiles[:, here] = total.astype(out.dtype)
            part = pl.ds(tile * width, width)
            copies.append(pltpu.make_async_copy(tiles.at[:, part], out.at[:, part], sem.at[tile]))
            copies[-1].start()
        else:
            out[:, here] = total
    for copy in copies:
        copy.wait()


def out_product(lefts, rights, partial, dtype):
    rows, width = lefts[0].shape[0], rights[0][0].shape[1]
    operands = list(lefts) + [pltpu.with_memory_space_constraint(w, pltpu.VMEM) for group in rights for w in group]
    if partial is not None:
        operands.append(partial)
    streamed = dtype == BF16
    return pl.pallas_call(
        functools.partial(out_kernel, len(rights[0])),
        in_specs=[VMEM] * len(operands),
        out_specs=HBM if streamed else VMEM,
        out_shape=jax.ShapeDtypeStruct((rows, width), dtype) if streamed else pltpu.VMEM((rows, width), dtype),
        scratch_shapes=[pltpu.VMEM((rows, width), dtype), pltpu.SemaphoreType.DMA((width // TILE,))] if streamed else [],
        compiler_params=params(8),
        cost_estimate=pl.CostEstimate(flops=COST, bytes_accessed=COST, transcendentals=0),
        name="out",
    )(*operands)


def swap(value, axis, bit):
    count = lax.axis_size(axis)
    return lax.ppermute(value, axis, [(i, i ^ bit) for i in range(count)])


def nothing(*_):
    pass


def after(value, earlier):
    return pl.pallas_call(
        nothing,
        in_specs=[pl.BlockSpec(memory_space=pl.ANY)] * 2,
        out_specs=pl.BlockSpec(memory_space=pl.ANY),
        out_shape=jax.ShapeDtypeStruct(value.shape, value.dtype),
        input_output_aliases={0: 0},
        compiler_params=params(1),
        cost_estimate=pl.CostEstimate(flops=COST, bytes_accessed=COST, transcendentals=0),
        name="after",
    )(value, earlier)


def local_call(kernel, name, operands, specs, outs, **kwargs):
    return pl.pallas_call(
        kernel,
        in_specs=specs,
        out_specs=[VMEM] * len(outs),
        out_shape=[pltpu.VMEM(shape, dtype) for shape, dtype in outs],
        cost_estimate=pl.CostEstimate(flops=FLOPS.get(name, COST), bytes_accessed=COST, transcendentals=0),
        compiler_params=params(VMEM_MIB[name]),
        name=name,
        **kwargs,
    )(*operands)


FLOPS = dict(keys=10**10, queries=3 * 10**8)
VMEM_MIB = dict(join=4, cut=4, keys=12, queries=12, group=8, scan=8, last=8, finish=8)


def prefix(place, own, received, message, others):
    count = lax.axis_size("seq")
    wide, thin = (own.shape, F32), (message.shape, BF16)
    step = QUAD
    before = []
    while True:
        late = lax.ppermute(message, "seq", [(i, i + step) for i in range(count - step)])
        step *= 2
        if step >= count:
            break
        earlier, message = local_call(
            functools.partial(scan_kernel, len(before)),
            "scan",
            [message, late] + before,
            [VMEM] * (2 + len(before)),
            [wide, thin],
        )
        before = [earlier]
    return local_call(
        functools.partial(last_kernel, len(before)),
        "last",
        [place, own] + received + [late] + before + others,
        [SMEM] + [VMEM] * (QUAD + 1 + len(before)) + [ANY] * len(others),
        [thin] * QUAD,
    )


def shards(tokens, w_query, w_key, w_value, omega, w_out):
    rows, width = tokens.shape
    size, feats = omega.shape
    heads = w_query.shape[1] // size
    blocks = rows // BLOCK
    seq_side = lax.axis_index("seq") % 2
    head_at = lax.axis_index("head")
    place = jnp.stack([seq_side, head_at, lax.axis_index("seq") % QUAD]).astype(jnp.int32)

    depth = w_out.shape[0] // 4
    (part,) = local_call(
        cut_kernel,
        "cut",
        [place, pltpu.with_memory_space_constraint(w_out, pltpu.HBM)],
        [SMEM, HBM],
        [((depth, w_out.shape[1]), BF16)],
        scratch_shapes=[pltpu.SemaphoreType.DMA],
    )
    near_part = swap(part, "head", 2)
    w_core = swap(w_out, "head", 1)

    group = heads // QUAD
    tok, wq, key_feat, value, own, *sent, local, rest = local_call(
        key_kernel,
        "keys",
        [place, pltpu.with_memory_space_constraint(tokens, pltpu.HBM), pltpu.with_memory_space_constraint(w_key, pltpu.VMEM)]
        + [pltpu.with_memory_space_constraint(v, pltpu.HBM) for v in (w_value, omega, w_query, w_out)]
        + [part],
        [SMEM, HBM, VMEM] + [HBM] * 4 + [ANY],
        [
            ((rows, width), BF16),
            (w_query.shape, BF16),
            ((heads, rows, feats), BF16),
            ((rows, heads * size), BF16),
            ((group, size + ROWS, feats), F32),
            ((group, size + 2 * ROWS, feats), BF16),
            ((group, size + 2 * ROWS, feats), BF16),
            ((group, size + 2 * ROWS, feats), BF16),
            ((max(blocks - 1, 1), heads, 2 * size, feats), BF16),
            ((w_out.shape[0] - 2 * depth, w_out.shape[1]), BF16),
        ],
        scratch_shapes=[
            pltpu.VMEM(w_value.shape, BF16),
            pltpu.VMEM(omega.shape, F32),
            pltpu.VMEM((rows, heads * size), F32),
            pltpu.SemaphoreType.DMA((9,)),
        ],
    )

    count = heads // 2

    def queries(first, others):
        return local_call(
            functools.partial(query_kernel, first, count),
            "queries",
            [tok, wq, omega, key_feat, value, local] + others,
            [VMEM] * 6 + [ANY] * len(others),
            [((count, rows, feats), BF16), ((rows, count * 2 * size), F32)],
            scratch_shapes=[pltpu.VMEM((rows, count * size), F32)],
        )

    received = [swap(v, "seq", k) for k, v in enumerate(sent, 1)]
    near_rest = swap(rest, "head", 2)
    partials = queries(0, [w_core])
    (message,) = local_call(
        group_kernel, "group", [own] + received + [partials[0], near_part], [VMEM] * QUAD + [ANY] * 2, [(sent[0].shape, BF16)]
    )
    near_part = after(near_part, message)
    partials = list(partials) + list(queries(count, [message]))
    far_part = swap(near_part, "seq", 1)
    kept, *handed = prefix(place, own, received, message, [partials[2]])
    prefixes = [kept] + [swap(v, "seq", k) for k, v in enumerate(handed, 1)]
    (joined,) = local_call(
        join_kernel,
        "join",
        [place, near_part, far_part],
        [SMEM] + [VMEM] * 2,
        [((2 * depth, w_out.shape[1]), BF16)],
    )

    share = rows // lax.axis_size("head")
    bits = (2, 3, 1, 0)
    to_x, to_diagonal, to_core, mine = local_call(
        functools.partial(finish_kernel, bits, count),
        "finish",
        [place] + prefixes + partials + [joined],
        [SMEM] + [VMEM] * (QUAD + len(partials)) + [ANY],
        [((share, heads * size), BF16)] * len(bits),
    )
    from_x = swap(to_x, "head", 2)
    from_diagonal = swap(to_diagonal, "head", 3)
    from_core = swap(to_core, "head", 1)

    total = out_product([mine, from_core], [[w_out], [w_core]], None, F32)
    pieces = [after(v, to_x) for v in (joined, near_rest)]
    core_pieces = [swap(v, "head", 1) for v in pieces]
    return out_product([from_x, from_diagonal], [pieces, core_pieces], total, BF16)


def solution(mesh):
    placed = (
        P("seq", None),
        P(None, "head"),
        P(None, "head"),
        P(None, "head"),
        P(),
        P("head", None),
    )
    return jax.shard_map(
        shards, mesh=mesh, in_specs=placed, out_specs=P(("seq", "head"), None), check_vma=False
    )
```

```python
import functools
import math

import jax
import jax.numpy as jnp
from jax import lax
from jax.experimental import pallas as pl
from jax.experimental.pallas import tpu as pltpu
from jax.sharding import PartitionSpec as P

BLOCK = 512
PART = 128
COST = 1000
QUAD = 4
TILE = 512
TAIL = 16
STABILIZER = 0.001
BF16 = jnp.bfloat16
F32 = jnp.float32


def params(mib):
    return pltpu.CompilerParams(vmem_limit_bytes=mib * 2**20)


def dot(a, b):
    return lax.dot_general(a, b, (((1,), (0,)), ((), ())), preferred_element_type=F32)


def dot_nt(a, b):
    return lax.dot_general(a, b, (((1,), (1,)), ((), ())), preferred_element_type=F32)


def dot_tn(a, b):
    return lax.dot_general(a, b, (((0,), (0,)), ((), ())), preferred_element_type=F32)


def halves(value):
    high = value.astype(BF16)
    return high, (value - high.astype(F32)).astype(BF16)


def feature_weights(omega):
    size, features = omega.shape
    high, low = halves(omega * size ** (-0.25))
    return jnp.concatenate([high, high, low, jnp.full((size, features), -1.0, BF16)], axis=0)


def features(rows, weights):
    size = rows.shape[1]
    high, low = halves(rows)
    squares = rows * rows * (0.5 * size ** (-0.5))
    squares = squares + pltpu.roll(squares, size // 2, 1)
    square_high, square_low = halves(squares)
    first = lax.broadcasted_iota(jnp.int32, rows.shape, 1) < size // 2
    square = jnp.where(first, square_high.astype(F32), square_low.astype(F32)).astype(BF16)
    exponent = dot(jnp.concatenate([high, low, high, square], axis=1), weights)
    return ((jnp.exp(exponent) + STABILIZER) * (1.0 / math.sqrt(weights.shape[1]))).astype(BF16)


VMEM = pl.BlockSpec(memory_space=pltpu.VMEM)
SMEM = pl.BlockSpec(memory_space=pltpu.SMEM)
HBM = pl.BlockSpec(memory_space=pltpu.HBM)
ANY = pl.BlockSpec(memory_space=pl.ANY)
ROWS = 8


def narrow(state):
    size = state.shape[0] - ROWS
    norm = state[size:]
    high = norm.astype(BF16).astype(F32)
    return jnp.concatenate([state[:size], high, norm - high], axis=0).astype(BF16)


def widen(message):
    size = message.shape[0] - 2 * ROWS
    wide = message.astype(F32)
    return jnp.concatenate([wide[:size], wide[size : size + ROWS] + wide[size + ROWS :]], axis=0)


def cut_kernel(place, whole, part, sem):
    depth = part.shape[0]
    start = pl.multiple_of(place[0] * depth, depth)
    copy = pltpu.make_async_copy(whole.at[pl.ds(start, depth)], part, sem)
    copy.start()
    copy.wait()


def key_kernel(
    place, tok, wk, wv, omega, wq, wo, _, tok_out, wq_out, feat, value, own, sent_1, sent_2, sent_3, local, rest, wv_in, om_in, keys, sem
):
    rows = tok.shape[0]
    size = omega.shape[0]
    chunk = rows // 4
    member = place[2]
    copies = []

    def fetch(source, target):
        copy = pltpu.make_async_copy(source, target, sem.at[len(copies)])
        copy.start()
        copies.append(copy)
        return copy

    def token_chunk(i):
        part = pl.ds(i * chunk, chunk)
        return fetch(tok.at[part], tok_out.at[part])

    token_copies = [token_chunk(0), token_chunk(1)]
    om_copy = fetch(omega, om_in)
    token_copies += [token_chunk(2), token_chunk(3)]
    wv_copy = fetch(wv, wv_in)
    wq_copy = fetch(wq, wq_out)
    rest_copy = fetch(wo.at[pl.ds(wo.shape[0] - rest.shape[0], rest.shape[0])], rest)

    for i, copy in enumerate(token_copies):
        copy.wait()
        part = slice(i * chunk, (i + 1) * chunk)
        keys[part] = dot(tok_out[part], wk[...])
    wv_copy.wait()
    for start in range(0, rows, BLOCK):
        part = slice(start, start + BLOCK)
        value[part] = dot(tok_out[part], wv_in[...]).astype(BF16)
    om_copy.wait()
    weights = feature_weights(om_in[...])
    ones = jnp.ones((BLOCK, TAIL), BF16)
    heads = feat.shape[0]
    for h in range(heads):
        columns = slice(h * size, (h + 1) * size)
        for start in range(0, rows, PART):
            part = slice(start, start + PART)
            feat[h, part] = features(keys[part, columns], weights)
    for h in range(heads):
        columns = slice(h * size, (h + 1) * size)
        total = None
        for block in range(rows // BLOCK):
            part = slice(block * BLOCK, (block + 1) * BLOCK)
            if block > 0:
                norm = jnp.broadcast_to(total[size : size + 1], (size, total.shape[1]))
                local[block - 1, h] = jnp.concatenate([total[:size], norm], axis=0).astype(BF16)
            added = dot_tn(jnp.concatenate([value[part, columns], ones], axis=1), feat[h, part])[: size + ROWS]
            total = added if total is None else total + added
        group = heads // QUAD

        @pl.when(member == h // group)
        def _():
            own[h % group] = total

        @pl.when(member != h // group)
        def _():
            thin = narrow(total)
            for k, sent in ((1, sent_1), (2, sent_2), (3, sent_3)):

                @pl.when(member ^ k == h // group)
                def _():
                    sent[h % group] = thin

    wq_copy.wait()
    rest_copy.wait()


def query_kernel(first, count, tok, wq, omega, feat, value, local, *rest):
    qfeat, result, query = rest[-3:]
    rows = tok.shape[0]
    size = omega.shape[0]
    half = BLOCK // 2
    weights = feature_weights(omega[...])
    causal = lax.broadcasted_iota(jnp.int32, (half, half), 0) >= lax.broadcasted_iota(
        jnp.int32, (half, half), 1
    )
    for start in range(0, rows, BLOCK):
        part = slice(start, start + BLOCK)
        query[part] = dot(tok[part], wq[:, first * size : (first + count) * size])
    for h in range(count):
        for start in range(0, rows, PART):
            part = slice(start, start + PART)
            qfeat[h, part] = features(query[part, h * size : (h + 1) * size], weights)
    for h in range(count):
        for block in range(rows // BLOCK):
            part = slice(block * BLOCK, (block + 1) * BLOCK)
            f = qfeat[h, part]
            k = feat[first + h, part]
            v = value[part, (first + h) * size : (first + h + 1) * size]
            v = jnp.concatenate([v, jnp.ones((BLOCK, size), BF16)], axis=1)
            top = jnp.where(causal, dot_nt(f[:half], k[:half]), 0.0).astype(BF16)
            left = dot_nt(f[half:], k[:half]).astype(BF16)
            right = jnp.where(causal, dot_nt(f[half:], k[half:]), 0.0).astype(BF16)
            upper = dot(top, v[:half])
            lower = dot(jnp.concatenate([left, right], axis=1), v)
            out = jnp.concatenate([upper, lower], axis=0)
            if block > 0:
                out = out + dot_nt(f, local[block - 1, first + h])
            result[part, h * 2 * size : (h + 1) * 2 * size] = out


def group_kernel(own, one, two, three, _, _2, sent):
    for j in range(own.shape[0]):
        sent[j] = narrow(own[j] + widen(one[j]) + widen(two[j]) + widen(three[j]))


def scan_kernel(count, message, received, *rest):
    before, (earlier, sent) = rest[:count], rest[-2:]
    for j in range(message.shape[0]):
        total = widen(received[j])
        if before:
            total = total + before[0][j]
        earlier[j] = total
        sent[j] = narrow(widen(message[j]) + total)


def last_kernel(count, place, own, one, two, three, late, *rest):
    before, outs = rest[:count], rest[-QUAD:]
    member = place[2]
    for j in range(own.shape[0]):
        total = widen(late[j])
        if before:
            total = total + before[0][j]
        states = [own[j], widen(one[j]), widen(two[j]), widen(three[j])]
        for k, out in enumerate(outs):
            value = total
            for i, state in enumerate(states):
                if i != k:
                    value = value + jnp.where((member ^ i) < (member ^ k), state, 0.0)
            out[j] = narrow(value)


def finish_kernel(bits, count, place, *refs):
    prefixes, partials, outs = refs[:QUAD], refs[QUAD:], refs[-len(bits) :]
    group = prefixes[0].shape[0]
    heads = QUAD * group
    size = outs[0].shape[1] // heads
    share = outs[0].shape[0]
    for h in range(heads):
        qfeat, result = partials[2 * (h // count)], partials[2 * (h // count) + 1]
        j = h % count
        p = prefixes[0][h % group].astype(F32)
        for k in range(1, QUAD):
            p = jnp.where(place[2] ^ k == h // group, prefixes[k][h % group].astype(F32), p)
        norm = p[size : size + 1] + p[size + ROWS : size + ROWS + 1]
        right = jnp.concatenate([p[:size], jnp.broadcast_to(norm, (size, p.shape[1]))], axis=0).astype(BF16)
        for bit, out in zip(bits, outs):
            part = pl.ds(pl.multiple_of((place[1] ^ bit) * share, share), share)
            r = result[part, j * 2 * size : (j + 1) * 2 * size] + dot_nt(qfeat[j, part, :], right)
            out[:, h * size : (h + 1) * size] = (r[:, :size] / r[:, size:]).astype(BF16)


def join_kernel(place, near, far, out):
    depth = near.shape[0]
    even = place[0] == 0
    out[:depth] = jnp.where(even, near[...], far[...])
    out[depth:] = jnp.where(even, far[...], near[...])


def out_kernel(count, *refs):
    lefts, rights, others = refs[:2], refs[2 : 2 + 2 * count], refs[2 + 2 * count :]
    streamed = len(others) > 2
    if streamed:
        before, out, tiles, sem = others
    else:
        (out,) = others
        before = None
    width = min(TILE, out.shape[1])
    copies = []
    for tile in range(out.shape[1] // width):
        here = slice(tile * width, (tile + 1) * width)
        total = before[:, here] if streamed else None
        for i, left in enumerate(lefts):
            parts = [ref[:, here] for ref in rights[count * i : count * (i + 1)]]
            term = dot(left[...], jnp.concatenate(parts, axis=0) if count > 1 else parts[0])
            total = term if total is None else total + term
        if streamed:
            tiles[:, here] = total.astype(out.dtype)
            part = pl.ds(tile * width, width)
            copies.append(pltpu.make_async_copy(tiles.at[:, part], out.at[:, part], sem.at[tile]))
            copies[-1].start()
        else:
            out[:, here] = total
    for copy in copies:
        copy.wait()


def out_product(lefts, rights, partial, dtype):
    rows, width = lefts[0].shape[0], rights[0][0].shape[1]
    operands = list(lefts) + [pltpu.with_memory_space_constraint(w, pltpu.VMEM) for group in rights for w in group]
    if partial is not None:
        operands.append(partial)
    streamed = dtype == BF16
    return pl.pallas_call(
        functools.partial(out_kernel, len(rights[0])),
        in_specs=[VMEM] * len(operands),
        out_specs=HBM if streamed else VMEM,
        out_shape=jax.ShapeDtypeStruct((rows, width), dtype) if streamed else pltpu.VMEM((rows, width), dtype),
        scratch_shapes=[pltpu.VMEM((rows, width), dtype), pltpu.SemaphoreType.DMA((width // TILE,))] if streamed else [],
        compiler_params=params(8),
        cost_estimate=pl.CostEstimate(flops=COST, bytes_accessed=COST, transcendentals=0),
        name="out",
    )(*operands)


def swap(value, axis, bit):
    count = lax.axis_size(axis)
    return lax.ppermute(value, axis, [(i, i ^ bit) for i in range(count)])


def nothing(*_):
    pass


def after(value, earlier):
    return pl.pallas_call(
        nothing,
        in_specs=[pl.BlockSpec(memory_space=pl.ANY)] * 2,
        out_specs=pl.BlockSpec(memory_space=pl.ANY),
        out_shape=jax.ShapeDtypeStruct(value.shape, value.dtype),
        input_output_aliases={0: 0},
        compiler_params=params(1),
        cost_estimate=pl.CostEstimate(flops=COST, bytes_accessed=COST, transcendentals=0),
        name="after",
    )(value, earlier)


def local_call(kernel, name, operands, specs, outs, **kwargs):
    return pl.pallas_call(
        kernel,
        in_specs=specs,
        out_specs=[VMEM] * len(outs),
        out_shape=[pltpu.VMEM(shape, dtype) for shape, dtype in outs],
        cost_estimate=pl.CostEstimate(flops=FLOPS.get(name, COST), bytes_accessed=COST, transcendentals=0),
        compiler_params=params(VMEM_MIB[name]),
        name=name,
        **kwargs,
    )(*operands)


FLOPS = dict(keys=10**10, queries=3 * 10**8)
VMEM_MIB = dict(join=4, cut=4, keys=12, queries=12, group=8, scan=8, last=8, finish=8)


def prefix(place, own, received, message, others):
    count = lax.axis_size("seq")
    wide, thin = (own.shape, F32), (message.shape, BF16)
    step = QUAD
    before = []
    while True:
        late = lax.ppermute(message, "seq", [(i, i + step) for i in range(count - step)])
        step *= 2
        if step >= count:
            break
        earlier, message = local_call(
            functools.partial(scan_kernel, len(before)),
            "scan",
            [message, late] + before,
            [VMEM] * (2 + len(before)),
            [wide, thin],
        )
        before = [earlier]
    return local_call(
        functools.partial(last_kernel, len(before)),
        "last",
        [place, own] + received + [late] + before + others,
        [SMEM] + [VMEM] * (QUAD + 1 + len(before)) + [ANY] * len(others),
        [thin] * QUAD,
    )


def shards(tokens, w_query, w_key, w_value, omega, w_out):
    rows, width = tokens.shape
    size, feats = omega.shape
    heads = w_query.shape[1] // size
    blocks = rows // BLOCK
    seq_side = lax.axis_index("seq") % 2
    head_at = lax.axis_index("head")
    place = jnp.stack([seq_side, head_at, lax.axis_index("seq") % QUAD]).astype(jnp.int32)

    depth = w_out.shape[0] * 7 // 32
    (part,) = local_call(
        cut_kernel,
        "cut",
        [place, pltpu.with_memory_space_constraint(w_out, pltpu.HBM)],
        [SMEM, HBM],
        [((depth, w_out.shape[1]), BF16)],
        scratch_shapes=[pltpu.SemaphoreType.DMA],
    )
    near_part = swap(part, "head", 2)
    w_core = swap(w_out, "head", 1)

    group = heads // QUAD
    tok, wq, key_feat, value, own, *sent, local, rest = local_call(
        key_kernel,
        "keys",
        [place, pltpu.with_memory_space_constraint(tokens, pltpu.HBM), pltpu.with_memory_space_constraint(w_key, pltpu.VMEM)]
        + [pltpu.with_memory_space_constraint(v, pltpu.HBM) for v in (w_value, omega, w_query, w_out)]
        + [part],
        [SMEM, HBM, VMEM] + [HBM] * 4 + [ANY],
        [
            ((rows, width), BF16),
            (w_query.shape, BF16),
            ((heads, rows, feats), BF16),
            ((rows, heads * size), BF16),
            ((group, size + ROWS, feats), F32),
            ((group, size + 2 * ROWS, feats), BF16),
            ((group, size + 2 * ROWS, feats), BF16),
            ((group, size + 2 * ROWS, feats), BF16),
            ((max(blocks - 1, 1), heads, 2 * size, feats), BF16),
            ((w_out.shape[0] - 2 * depth, w_out.shape[1]), BF16),
        ],
        scratch_shapes=[
            pltpu.VMEM(w_value.shape, BF16),
            pltpu.VMEM(omega.shape, F32),
            pltpu.VMEM((rows, heads * size), F32),
            pltpu.SemaphoreType.DMA((9,)),
        ],
    )

    count = heads // 2

    def queries(first, others):
        return local_call(
            functools.partial(query_kernel, first, count),
            "queries",
            [tok, wq, omega, key_feat, value, local] + others,
            [VMEM] * 6 + [ANY] * len(others),
            [((count, rows, feats), BF16), ((rows, count * 2 * size), F32)],
            scratch_shapes=[pltpu.VMEM((rows, count * size), F32)],
        )

    received = [swap(v, "seq", k) for k, v in enumerate(sent, 1)]
    near_rest = swap(rest, "head", 2)
    partials = queries(0, [w_core])
    (message,) = local_call(
        group_kernel, "group", [own] + received + [partials[0], near_part], [VMEM] * QUAD + [ANY] * 2, [(sent[0].shape, BF16)]
    )
    near_part = after(near_part, message)
    partials = list(partials) + list(queries(count, [message]))
    far_part = swap(near_part, "seq", 1)
    kept, *handed = prefix(place, own, received, message, [partials[2]])
    prefixes = [kept] + [swap(v, "seq", k) for k, v in enumerate(handed, 1)]
    (joined,) = local_call(
        join_kernel,
        "join",
        [place, near_part, far_part],
        [SMEM] + [VMEM] * 2,
        [((2 * depth, w_out.shape[1]), BF16)],
    )

    share = rows // lax.axis_size("head")
    bits = (2, 3, 1, 0)
    to_x, to_diagonal, to_core, mine = local_call(
        functools.partial(finish_kernel, bits, count),
        "finish",
        [place] + prefixes + partials + [joined],
        [SMEM] + [VMEM] * (QUAD + len(partials)) + [ANY],
        [((share, heads * size), BF16)] * len(bits),
    )
    from_x = swap(to_x, "head", 2)
    from_diagonal = swap(to_diagonal, "head", 3)
    from_core = swap(to_core, "head", 1)

    total = out_product([mine, from_core], [[w_out], [w_core]], None, F32)
    pieces = [after(v, to_x) for v in (joined, near_rest)]
    core_pieces = [swap(v, "head", 1) for v in pieces]
    return out_product([from_x, from_diagonal], [pieces, core_pieces], total, BF16)


def solution(mesh):
    placed = (
        P("seq", None),
        P(None, "head"),
        P(None, "head"),
        P(None, "head"),
        P(),
        P("head", None),
    )
    return jax.shard_map(
        shards, mesh=mesh, in_specs=placed, out_specs=P(("seq", "head"), None), check_vma=False
    )
```
